512 devices in a mesh: dp: 4 (over y), tm: 16 (over z), height: 8 (over x, core).
Axes of the slice: x: 4, y: 4, z: 16, core: 2. Of those that a mesh axis runs over, the one named last changes fastest.
Arguments:
- inputs: bfloat16 [4, 32, 16, 40, 256], P('dp', 'tm', 'height'), may hold values from -240 to 240
- grad_out: bfloat16 [4, 32, 16, 40, 256], P('dp', 'tm', 'height'), may hold values from -215 to 215
- conv1_weight: bfloat16 [3, 9, 256, 256], P(None, None, ('dp', 'height')), may hold values from -0.078125 to 0.078125
- conv2_weight: bfloat16 [3, 9, 256, 256], P(None, None, ('dp', 'height')), may hold values from -0.078125 to 0.078125
- gain1: float32 [256], replicated, may hold values from 0.1 to 1.9
- shift1: float32 [256], replicated, may hold values from -3 to 3
- gain2: float32 [256], replicated, may hold values from 0.1 to 1.9
- shift2: float32 [256], replicated, may hold values from -3 to 3
Outputs:
- grad_in: bfloat16 [4, 32, 16, 40, 256], P('dp', 'tm', 'height')
The draws below stay inside these ranges and needn't reach their ends.
All inputs are finite; a program needn't handle non-finite values.
Results may differ from the reference program's by a relative error of at most 0.0045.
Values may be sent and summed in bfloat16 or wider, within the bound.
No kernel may reach another device: no remote copies, remote signals or barrier semaphores. Data moves between devices by JAX's collectives and lax.ppermute only.
A program may use at most 64 MiB of HBM per device.

```python
import jax
import jax.numpy as jnp
from jax import lax

CHANNELS = 256
GROUPS = 32
COLS = 40
CLIPS = 4
FRAMES = 32
ROWS = 16


def ramp_field(shape):
    frame_pos = lax.broadcasted_iota(jnp.float32, shape, 1) / max(FRAMES - 1, 1)
    row_pos = lax.broadcasted_iota(jnp.float32, shape, 2) / max(ROWS - 1, 1)
    return jnp.exp(jnp.log(4.5) * (frame_pos + row_pos))


def level_field(key):
    keys = jax.random.split(key, 2)
    frame_level = jnp.exp(jax.random.uniform(keys[0], (CLIPS, FRAMES, 1, 1, 1), jnp.float32, -0.4, 0.0))
    row_level = jnp.exp(jax.random.uniform(keys[1], (CLIPS, 1, ROWS, 1, 1), jnp.float32, -0.4, 0.0))
    return frame_level * row_level


def field_draw(key, offset_scale):
    shape = (CLIPS, FRAMES, ROWS, COLS, CHANNELS)
    keys = jax.random.split(key, 5)
    channel_scale = jnp.exp(jax.random.uniform(keys[0], (CHANNELS,), jnp.float32, jnp.log(0.2), jnp.log(2.0)))
    rough = jax.random.uniform(keys[1], shape, jnp.float32, 0.5, 1.05)
    base = jax.random.truncated_normal(keys[2], -4.0, 4.0, shape, jnp.float32)
    offset = offset_scale * jax.random.truncated_normal(keys[3], -3.0, 3.0, (CHANNELS,), jnp.float32)
    return (base + offset) * channel_scale * ramp_field(shape) * level_field(keys[4]) * rough


def draw_inputs(key, part):
    key = jax.random.fold_in(key, 11)
    return field_draw(key, 0.5).astype(jnp.bfloat16)


def draw_grad_out(key, part):
    key = jax.random.fold_in(key, 23)
    return field_draw(key, 0.3).astype(jnp.bfloat16)


def shard_levels(own_key, extent, shards, low, top_value):
    factor_of = 1.0
    for position, parts in shards:
        heights = jax.random.uniform(jax.random.fold_in(jax.random.fold_in(own_key, 6), position), (parts,), jnp.float32, low / len(shards), top_value / len(shards))
        factor_of = factor_of * jnp.repeat(jnp.exp(heights), extent[position] // parts).reshape((-1,) + (1,) * (len(extent) - 1 - position))
    return factor_of


def noise(stream_key, shape, deviation, bound, pieces=(), held_as=jnp.bfloat16):
    values = deviation * jax.random.normal(stream_key, shape, jnp.float32)
    if pieces:
        values = values * shard_levels(stream_key, shape, pieces, -0.22, 0.18)
    return jnp.clip(values, -bound, bound).astype(held_as)


def setup_inputs(seed: int = 0) -> dict:
    streams_of = jax.random.split(jax.random.key(seed), 9)
    inputs = draw_inputs(jax.random.fold_in(streams_of[8], 71), 0)
    grad_out = draw_grad_out(jax.random.fold_in(streams_of[8], 71), 0)
    conv1_weight = noise(streams_of[2], (3, 9, CHANNELS, CHANNELS), (27 * CHANNELS) ** -0.5, 0.078125, ((2, 32),))
    conv2_weight = noise(streams_of[3], (3, 9, CHANNELS, CHANNELS), (27 * CHANNELS) ** -0.5, 0.078125, ((2, 32),))
    gain1 = jnp.clip(1.0 + 0.18 * jax.random.normal(streams_of[4], (CHANNELS,), jnp.float32), 0.1, 1.9)
    shift1 = noise(streams_of[5], (CHANNELS,), 0.5, 3.0, (), jnp.float32)
    gain2 = jnp.clip(1.0 + 0.18 * jax.random.normal(streams_of[6], (CHANNELS,), jnp.float32), 0.1, 1.9)
    shift2 = noise(streams_of[7], (CHANNELS,), 0.5, 3.0, (), jnp.float32)
    return {"inputs": inputs, "grad_out": grad_out, "conv1_weight": conv1_weight, "conv2_weight": conv2_weight, "gain1": gain1, "shift1": shift1, "gain2": gain2, "shift2": shift2}


norm_eps = 1e-06

def silu_slope(value):
    sigma = jax.nn.sigmoid(value)
    return sigma * (1.0 + value * (1.0 - sigma))

def conv_forward(volume, weight):
    kernel = weight.astype(jnp.float32).reshape(3, 3, 3, CHANNELS, CHANNELS)
    result = lax.conv_general_dilated(volume[None], kernel, (1, 1, 1), ((2, 0), (1, 1), (1, 1)), dimension_numbers=('NDHWC', 'DHWIO', 'NDHWC'), precision=lax.Precision.HIGHEST)
    return result[0]

def conv_backward(cotangent, weight):
    _, pull = jax.vjp(lambda volume: conv_forward(volume, weight), jnp.zeros_like(cotangent))
    return pull(cotangent)[0]

def moments(volume):
    width = CHANNELS // GROUPS
    grouped = volume.reshape(FRAMES, ROWS, COLS, GROUPS, width)
    mean = lax.optimization_barrier(jnp.mean(grouped, axis=(0, 1, 2, 4), keepdims=True))
    variance = lax.optimization_barrier(jnp.mean((grouped - mean) ** 2, axis=(0, 1, 2, 4), keepdims=True))
    inv_std = 1.0 / jnp.sqrt(variance + norm_eps)
    normed = ((grouped - mean) * inv_std).reshape(volume.shape)
    return (normed, jnp.repeat(inv_std.reshape(GROUPS), width))

def norm_grad(slope, normed, inv_std):
    width = CHANNELS // GROUPS
    grouped_slope = slope.reshape(FRAMES, ROWS, COLS, GROUPS, width)
    grouped_normed = normed.reshape(FRAMES, ROWS, COLS, GROUPS, width)
    first = lax.optimization_barrier(jnp.mean(grouped_slope, axis=(0, 1, 2, 4), keepdims=True))
    second = lax.optimization_barrier(jnp.mean(grouped_slope * grouped_normed, axis=(0, 1, 2, 4), keepdims=True))
    inner = (grouped_slope - first - grouped_normed * second).reshape(slope.shape)
    return inv_std * inner

def reference(inputs, grad_out, conv1_weight, conv2_weight, gain1, shift1, gain2, shift2):

    def one_clip(pair):
        input_clip, grad_clip = pair
        values = input_clip.astype(jnp.float32)
        normed1, inv1 = moments(values)
        pre1 = normed1 * gain1 + shift1
        act1 = jax.nn.silu(pre1).astype(jnp.bfloat16)
        hidden = conv_forward(act1.astype(jnp.float32), conv1_weight).astype(jnp.bfloat16)
        hidden = lax.optimization_barrier(hidden).astype(jnp.float32)
        normed2, inv2 = moments(hidden)
        pre2 = normed2 * gain2 + shift2
        grad_act2 = conv_backward(grad_clip.astype(jnp.float32), conv2_weight)
        slope2 = grad_act2 * silu_slope(pre2) * gain2
        grad_hidden = norm_grad(slope2, normed2, inv2).astype(jnp.bfloat16)
        grad_hidden = lax.optimization_barrier(grad_hidden).astype(jnp.float32)
        grad_act1 = conv_backward(grad_hidden, conv1_weight)
        slope1 = grad_act1 * silu_slope(pre1) * gain1
        return (grad_clip.astype(jnp.float32) + norm_grad(slope1, normed1, inv1)).astype(jnp.bfloat16)
    return lax.map(one_clip, (inputs, grad_out))
```

```python
import jax
import jax.numpy as jnp
import numpy as np
from jax import lax
from jax.experimental import pallas as pl
from jax.experimental.pallas import tpu as pltpu
from jax.sharding import PartitionSpec as P

EPS = 1e-06
F32 = jnp.float32
BF16 = jnp.bfloat16
CH = 256
OWN = 32
COLS = 40
IMG = 640
POS = 2 * IMG
SHARD = 160
PART = 80
COUNT = 32 * IMG * 8


def iota(shape, dim):
    return lax.broadcasted_iota(jnp.int32, shape, dim)


def exact(a, b, dims):
    return lax.dot_general(
        a, b, (dims, ((), ())), precision=lax.Precision.HIGHEST, preferred_element_type=F32
    )


def mm(a, b, dims):
    return lax.dot_general(a, b, (dims, ((), ())), preferred_element_type=F32)


NT = ((1,), (1,))
NN = ((1,), (0,))
TN = ((0,), (0,))


def channel_of(index):
    return ((index >> 3) & 3) * 64 + (index >> 5) * 8 + (index & 7)


def order_matrix():
    return (iota((CH, CH), 1) == channel_of(iota((CH, CH), 0))).astype(F32).astype(BF16)


def own_matrix(h):
    place = iota((OWN, CH), 0)
    return (iota((OWN, CH), 1) == (place >> 3) * 64 + h * 8 + (place & 7)).astype(F32)


def call(kernel, outs, *args, smem=0, flops=10**7):
    many = isinstance(outs, (list, tuple))
    specs = [pl.BlockSpec(memory_space=pltpu.SMEM)] * smem
    specs += [pl.BlockSpec(memory_space=pltpu.VMEM)] * (len(args) - smem)
    vmem = pl.BlockSpec(memory_space=pltpu.VMEM)
    return pl.pallas_call(
        kernel,
        out_shape=outs,
        in_specs=specs,
        out_specs=[vmem] * len(outs) if many else vmem,
        compiler_params=pltpu.CompilerParams(vmem_limit_bytes=32 * 2**20),
        cost_estimate=pl.CostEstimate(flops=flops, bytes_accessed=10**6, transcendentals=0),
    )(*args)


def shape(*dims, dtype=F32):
    return jax.ShapeDtypeStruct(dims, dtype)


def spread(block, axis, count):
    return lax.all_to_all(
        jnp.broadcast_to(block[None], (count,) + block.shape), axis, 0, 0, tiled=True
    )


def to_later(block):
    size = lax.axis_size("tm")
    return lax.ppermute(block, "tm", [(i, i + 1) for i in range(size - 1)])


def to_earlier(block):
    size = lax.axis_size("tm")
    return lax.ppermute(block, "tm", [(i + 1, i) for i in range(size - 1)])


def first_stats(x_ref, row_ref):
    x = x_ref[...].astype(F32)
    same = ((iota((CH, CH), 0) >> 3) == (iota((CH, CH), 1) >> 3)).astype(F32)
    group = iota((CH, 128), 0) >> 3
    lane = iota((CH, 128), 1)
    sums = jnp.sum(x, axis=0, keepdims=True)
    mean = exact(jnp.broadcast_to(sums, (8, CH)), same, NN)[:1] * (1.0 / (SHARD * 8))
    centred = x - mean
    squares = jnp.sum(centred * centred, axis=0, keepdims=True)
    means = exact(
        jnp.broadcast_to(mean, (8, CH)), ((group == lane) & ((iota((CH, 128), 0) & 7) == 0)).astype(F32), NN
    )
    spreads = exact(jnp.broadcast_to(squares, (8, CH)), (group + 32 == lane).astype(F32), NN)
    row_ref[...] = (means + spreads)[:1]


def cut_weight(w_ref, out_ref):
    total = None
    lane = iota((CH, 1024), 1)
    channel = ((lane >> 3) & 3) * 64 + (lane >> 7) * 8 + (lane & 7)
    hit = iota((CH, 1024), 0) == channel
    for a in range(4):
        place = (hit & (((lane >> 5) & 3) == a)).astype(F32).astype(BF16)
        term = mm(w_ref[a], place, NN)
        total = term if total is None else total + term
    for owner in range(8):
        out_ref[owner] = total[:, owner * 128 : owner * 128 + 128].astype(BF16)


def turn_weight(w_ref, out_ref):
    eye = (iota((128, 128), 0) == iota((128, 128), 1)).astype(F32).astype(BF16)
    for part in range(7):
        out_ref[part * 128 : part * 128 + 128, :] = mm(eye, w_ref[part], NT).astype(BF16)


def order_weight(w_ref, out_ref):
    out_ref[...] = mm(w_ref[...], order_matrix(), NT).astype(BF16)


def shifted(value, by, keep):
    return jnp.where(keep, pltpu.roll(value, (-by) % IMG, 1), 0.0)


def fold(taps, sign, cols_ref):
    lane = iota((OWN, IMG), 1)
    col = jnp.broadcast_to(cols_ref[...], (OWN, IMG))
    keep_col = {1: col != COLS - 1, -1: col != 0}
    keep_row = {1: lane < IMG - COLS, -1: lane >= COLS}
    total = None
    for j in range(3):
        line = None
        for k in range(3):
            value = taps[(3 * j + k) * OWN : (3 * j + k + 1) * OWN, :]
            step = sign * (k - 1)
            if step:
                value = shifted(value, step, keep_col[step])
            line = value if line is None else line + value
        step = sign * (j - 1)
        if step:
            line = shifted(line, step * COLS, keep_row[step])
        total = line if total is None else total + line
    return total


def convolve(frames, weight, dims, forward, cols_ref, own_ref, other_ref):
    if forward:
        plan = [(2, [(0, 0), (1, 1)], other_ref, 0), (3, [(1, 0)], other_ref, 1),
                (0, [(0, 2)], own_ref, 0), (1, [(0, 1), (1, 2)], own_ref, 1)]
    else:
        plan = [(-2, [(0, 0)], other_ref, 0), (-1, [(0, 1), (1, 0)], other_ref, 1),
                (0, [(0, 2), (1, 1)], own_ref, 0), (1, [(1, 2)], own_ref, 1)]
    for _, terms, ref, slot in plan:
        taps = None
        for frame, time_tap in terms:
            term = mm(weight[time_tap * 288 : time_tap * 288 + 288, :], frames[frame], dims)
            taps = term if taps is None else taps + term
        ref[:, slot * IMG : slot * IMG + IMG] = fold(taps, 1 if forward else -1, cols_ref)


def frame_of(ref, frame):
    return ref[:, frame * PART : frame * PART + PART, :].reshape(IMG, CH)


def first_conv(h_ref, stats_ref, x_ref, w_ref, vec_ref, cols_ref, own_ref, other_ref, normed_ref, column_ref):
    stats = stats_ref[...]
    lane = iota((128, 128), 1)
    mean = jnp.sum(stats, axis=0, keepdims=True) * (1.0 / 128)
    off = stats - mean
    spread_sum = jnp.sum(jnp.where(lane < 32, off * off * (SHARD * 8.0), stats), axis=0, keepdims=True)
    row = iota((8, 128), 0)
    lane8 = iota((8, 128), 1)
    both = jnp.where(row == 0, jnp.where(lane8 < 32, mean, 0.0), jnp.where(lane8 < 64, spread_sum, 0.0))
    expand = ((iota((128, CH), 0) & 31) == (iota((128, CH), 1) >> 3)).astype(F32)
    wide = exact(both, expand, NN)
    mean_c = wide[0:1]
    inv_c = lax.rsqrt(wide[1:2] * (1.0 / COUNT) + EPS)
    gain, shift = vec_ref[0:1], vec_ref[1:2]
    own = own_matrix(h_ref[0])
    row8 = iota((8, CH), 0)
    vectors = jnp.where(row8 == 4, mean_c, jnp.where(row8 == 5, inv_c, vec_ref[...]))
    columns = exact(own, vectors, NT)
    column_ref[...] = columns
    own16 = own.astype(BF16)
    acts = []
    for frame in range(2):
        raw = frame_of(x_ref, frame)
        normed_ref[:, frame * IMG : frame * IMG + IMG] = (mm(own16, raw, NT) - columns[:, 4:5]) * columns[:, 5:6]
        pre = (raw.astype(F32) - mean_c) * inv_c * gain + shift
        acts.append((pre * jax.nn.sigmoid(pre)).astype(BF16))
    convolve(acts, w_ref, NT, True, cols_ref, own_ref, other_ref)


def lanes_of(values):
    lane = iota((1, 128), 1)
    row = jnp.zeros((1, 128), F32)
    for n, value in enumerate(values):
        row = jnp.where(lane == n, value, row)
    return row


def lane_of(row, n):
    return jnp.sum(jnp.where(iota((1, 128), 1) == n, row, 0.0), axis=1, keepdims=True)


def total_of(value):
    return jnp.sum(jnp.sum(value, axis=1, keepdims=True), axis=0, keepdims=True)


def hidden_stats(own_ref, got_ref, hidden_ref, row_ref):
    means, spreads = [], []
    for g in range(4):
        rows = slice(8 * g, 8 * g + 8)
        value = (own_ref[rows, :] + got_ref[rows, :]).astype(BF16).astype(F32)
        hidden_ref[rows, :] = value
        mean = total_of(value) * (1.0 / (8 * POS))
        off = value - mean
        means.append(mean)
        spreads.append(total_of(off * off))
    row_ref[...] = lanes_of(means + spreads)


def silu_slope(value):
    sigma = jax.nn.sigmoid(value)
    return sigma * (1.0 + value * (1.0 - sigma))


def second_conv(h_ref, g_ref, w_ref, cols_ref, own_ref, other_ref, grad_ref):
    own16 = own_matrix(h_ref[0]).astype(BF16)
    frames = [frame_of(g_ref, frame) for frame in range(2)]
    convolve(frames, w_ref, NT, False, cols_ref, own_ref, other_ref)
    for frame in range(2):
        grad_ref[:, frame * IMG : frame * IMG + IMG] = mm(own16, frames[frame], NT)


def second_slope(stats_ref, hidden_ref, own_ref, got_ref, column_ref, slope_ref, normed_ref, inv_ref, row_ref):
    stats = stats_ref[...]
    mean_row = jnp.sum(stats, axis=0, keepdims=True) * (1.0 / 16)
    off = stats - mean_row
    between = jnp.sum(off * off, axis=0, keepdims=True) * (8.0 * POS)
    within = jnp.sum(stats, axis=0, keepdims=True)
    firsts, seconds, invs = [], [], []
    for g in range(4):
        rows = slice(8 * g, 8 * g + 8)
        mean = lane_of(mean_row, g)
        inv = lax.rsqrt((lane_of(between, g) + lane_of(within, 4 + g)) * (1.0 / COUNT) + EPS)
        normed = (hidden_ref[rows, :] - mean) * inv
        gain, shift = column_ref[rows, 2:3], column_ref[rows, 3:4]
        slope = (own_ref[rows, :] + got_ref[rows, :]) * silu_slope(normed * gain + shift) * gain
        slope_ref[rows, :] = slope
        normed_ref[rows, :] = normed
        firsts.append(total_of(slope))
        seconds.append(total_of(slope * normed))
        invs.append(inv)
    inv_ref[...] = lanes_of(invs)
    row_ref[...] = lanes_of(firsts + seconds)


def hidden_grad(sums_ref, slope_ref, normed_ref, inv_ref, out_ref):
    means = jnp.sum(sums_ref[...], axis=0, keepdims=True) * (1.0 / COUNT)
    values = []
    for g in range(4):
        rows = slice(8 * g, 8 * g + 8)
        inv = lane_of(inv_ref[...], g)
        values.append(
            inv * (slope_ref[rows, :] - lane_of(means, g) - normed_ref[rows, :] * lane_of(means, 4 + g))
        )
    out_ref[...] = jnp.concatenate(values, axis=0).astype(BF16)


def third_conv(g_ref, w_ref, cols_ref, own_ref, other_ref):
    frames = [
        g_ref[:, :, frame * IMG : frame * IMG + IMG].reshape(CH, IMG) for frame in range(2)
    ]
    convolve(frames, w_ref, NN, False, cols_ref, own_ref, other_ref)


def first_slope(own_ref, got_ref, normed_ref, column_ref, slope_ref, row_ref):
    firsts, seconds = [], []
    for g in range(4):
        rows = slice(8 * g, 8 * g + 8)
        normed = normed_ref[rows, :]
        gain, shift = column_ref[rows, 0:1], column_ref[rows, 1:2]
        slope = (own_ref[rows, :] + got_ref[rows, :]) * silu_slope(normed * gain + shift) * gain
        slope_ref[rows, :] = slope
        firsts.append(total_of(slope))
        seconds.append(total_of(slope * normed))
    row_ref[...] = lanes_of(firsts + seconds)


def input_grad(sums_ref, slope_ref, normed_ref, column_ref, grad_ref, out_ref):
    means = jnp.sum(sums_ref[...], axis=0, keepdims=True) * (1.0 / COUNT)
    values = []
    for g in range(4):
        rows = slice(8 * g, 8 * g + 8)
        inner = slope_ref[rows, :] - lane_of(means, g) - normed_ref[rows, :] * lane_of(means, 4 + g)
        values.append(grad_ref[rows, :] + column_ref[rows, 5:6] * inner)
    value = jnp.concatenate(values, axis=0)
    for frame in range(2):
        image = value[:, frame * IMG : frame * IMG + IMG]
        for owner in range(8):
            moved = pltpu.roll(image, (-owner * PART) % IMG, 1) if owner else image
            out_ref[owner, :, frame * 128 : frame * 128 + 128] = moved[:, :128].astype(BF16)


def gather_rows(got_ref, out_ref):
    order = order_matrix()
    for frame in range(2):
        value = got_ref[:, :, frame * 128 : frame * 128 + 128].reshape(CH, 128)
        out_ref[frame * PART : frame * PART + PART, :] = mm(value, order, TN)[:PART].astype(BF16)


def on_device(inputs, grad_out, conv1_weight, conv2_weight, gain1, shift1, gain2, shift2):
    x = inputs.reshape(SHARD, CH)
    upstream = grad_out.reshape(SHARD, CH)
    h = lax.axis_index("height").astype(jnp.int32).reshape(1)
    cols = jnp.asarray(np.arange(IMG)[None, :] % COLS, jnp.int32)
    zero = jnp.zeros_like(gain1)
    vectors = jnp.stack([gain1, shift1, gain2, shift2, zero, zero, zero, zero])
    half = shape(OWN, POS)
    row = shape(1, 128)

    stats1 = spread(call(first_stats, row, x), ("tm", "height"), 128).reshape(128, 128)
    x_all = spread(x, "height", 8)
    taps = jnp.pad(conv1_weight.reshape(27, 8, CH), ((0, 5), (0, 0), (0, 0)))
    taps = taps.reshape(8, 4, 8, CH).transpose(1, 0, 2, 3).reshape(4, 64, CH)
    pieces = call(cut_weight, shape(8, 64, 128, dtype=BF16), taps)
    pieces = jnp.broadcast_to(pieces[None], (4, 8, 64, 128)).reshape(32, 64, 128)
    pieces = lax.all_to_all(pieces, ("dp", "height"), 0, 0, tiled=True)
    pieces = pieces.reshape(32, 8, 8, 128).transpose(1, 0, 2, 3).reshape(8, CH, 128)
    w1_forward = call(turn_weight, shape(896, CH, dtype=BF16), pieces)
    g_all = spread(upstream, "height", 8)
    both = jnp.concatenate([conv2_weight.reshape(27, 8, CH), conv1_weight.reshape(27, 8, CH)])
    both = spread(both, "dp", 4)
    both = both.reshape(4, 2, 27, 8, CH).transpose(1, 2, 0, 3, 4).reshape(2, 864, CH)
    w2_back = both[0]
    w1_back = call(order_weight, shape(864, CH, dtype=BF16), both[1])

    own, other, normed1, columns = call(
        first_conv, [half, half, half, shape(OWN, 8)], h, stats1, x_all, w1_forward, vectors, cols, smem=1
    )
    got = to_later(other)
    hidden, stats2 = call(hidden_stats, [half, row], own, got)
    stats2 = spread(stats2, "tm", 16).reshape(16, 128)
    own, other, grad_t = call(second_conv, [half, half, half], h, g_all, w2_back, cols, smem=1)
    got = to_earlier(other)
    slope2, normed2, inv2, sums2 = call(
        second_slope, [half, half, row, row], stats2, hidden, own, got, columns
    )
    sums2 = spread(sums2, "tm", 16).reshape(16, 128)
    grad_hidden = call(hidden_grad, shape(OWN, POS, dtype=BF16), sums2, slope2, normed2, inv2)
    grad_hidden = spread(grad_hidden, "height", 8)
    own, other = call(third_conv, [half, half], grad_hidden, w1_back, cols)
    got = to_earlier(other)
    slope1, sums1 = call(first_slope, [half, row], own, got, normed1, columns)
    sums1 = spread(sums1, "tm", 16).reshape(16, 128)
    result = call(input_grad, shape(8, OWN, 256, dtype=BF16), sums1, slope1, normed1, columns, grad_t)
    result = lax.all_to_all(result, "height", 0, 0, tiled=True)
    return call(gather_rows, shape(SHARD, CH, dtype=BF16), result).reshape(inputs.shape)


def solution(mesh):
    return jax.shard_map(
        on_device,
        mesh=mesh,
        in_specs=(
            P("dp", "tm", "height", None, None),
            P("dp", "tm", "height", None, None),
            P(None, None, ("dp", "height"), None),
            P(None, None, ("dp", "height"), None),
            P(),
            P(),
            P(),
            P(),
        ),
        out_specs=P("dp", "tm", "height", None, None),
        check_vma=False,
    )
```

```python
import jax
import jax.numpy as jnp
import numpy as np
from jax import lax
from jax.experimental import pallas as pl
from jax.experimental.pallas import tpu as pltpu
from jax.sharding import PartitionSpec as P

EPS = 1e-06
F32 = jnp.float32
BF16 = jnp.bfloat16
CH = 256
OWN = 32
COLS = 40
IMG = 640
POS = 2 * IMG
SHARD = 160
PART = 80
COUNT = 32 * IMG * 8


def iota(shape, dim):
    return lax.broadcasted_iota(jnp.int32, shape, dim)


def exact(a, b, dims):
    return lax.dot_general(
        a, b, (dims, ((), ())), precision=lax.Precision.HIGHEST, preferred_element_type=F32
    )


def mm(a, b, dims):
    return lax.dot_general(a, b, (dims, ((), ())), preferred_element_type=F32)


NT = ((1,), (1,))
NN = ((1,), (0,))
TN = ((0,), (0,))


def channel_of(index):
    return ((index >> 3) & 3) * 64 + (index >> 5) * 8 + (index & 7)


def order_matrix():
    return (iota((CH, CH), 1) == channel_of(iota((CH, CH), 0))).astype(F32).astype(BF16)


def own_matrix(h):
    place = iota((OWN, CH), 0)
    return (iota((OWN, CH), 1) == (place >> 3) * 64 + h * 8 + (place & 7)).astype(F32)


def call(kernel, outs, *args, smem=0, flops=10**7):
    many = isinstance(outs, (list, tuple))
    specs = [pl.BlockSpec(memory_space=pltpu.SMEM)] * smem
    specs += [pl.BlockSpec(memory_space=pltpu.VMEM)] * (len(args) - smem)
    vmem = pl.BlockSpec(memory_space=pltpu.VMEM)
    return pl.pallas_call(
        kernel,
        out_shape=outs,
        in_specs=specs,
        out_specs=[vmem] * len(outs) if many else vmem,
        compiler_params=pltpu.CompilerParams(vmem_limit_bytes=32 * 2**20),
        cost_estimate=pl.CostEstimate(flops=flops, bytes_accessed=10**6, transcendentals=0),
    )(*args)


def shape(*dims, dtype=F32):
    return jax.ShapeDtypeStruct(dims, dtype)


def spread(block, axis, count):
    return lax.all_to_all(
        jnp.broadcast_to(block[None], (count,) + block.shape), axis, 0, 0, tiled=True
    )


def to_later(block):
    size = lax.axis_size("tm")
    return lax.ppermute(block, "tm", [(i, i + 1) for i in range(size - 1)])


def to_earlier(block):
    size = lax.axis_size("tm")
    return lax.ppermute(block, "tm", [(i + 1, i) for i in range(size - 1)])


def first_stats(x_ref, row_ref):
    frames = [frame_of(x_ref, frame).astype(F32) for frame in range(2)]
    same = ((iota((CH, CH), 0) >> 3) == (iota((CH, CH), 1) >> 3)).astype(F32)
    group = iota((CH, 128), 0) >> 3
    lane = iota((CH, 128), 1)
    sums = sum(jnp.sum(x, axis=0, keepdims=True) for x in frames)
    mean = exact(jnp.broadcast_to(sums, (8, CH)), same, NN)[:1] * (1.0 / (POS * 8))
    squares = sum(jnp.sum((x - mean) * (x - mean), axis=0, keepdims=True) for x in frames)
    means = exact(
        jnp.broadcast_to(mean, (8, CH)), ((group == lane) & ((iota((CH, 128), 0) & 7) == 0)).astype(F32), NN
    )
    spreads = exact(jnp.broadcast_to(squares, (8, CH)), (group + 32 == lane).astype(F32), NN)
    row_ref[...] = (means + spreads)[:1]


def first_parcel(x_ref, w_ref, out_ref):
    total = None
    lane = iota((CH, 1024), 1)
    channel = ((lane >> 3) & 3) * 64 + (lane >> 7) * 8 + (lane & 7)
    hit = iota((CH, 1024), 0) == channel
    for a in range(4):
        place = (hit & (((lane >> 5) & 3) == a)).astype(F32).astype(BF16)
        term = mm(w_ref[a], place, NN)
        total = term if total is None else total + term
    for owner in range(8):
        piece = total[:, owner * 128 : owner * 128 + 128].astype(BF16)
        out_ref[owner, :SHARD, :] = x_ref[...]
        out_ref[owner, SHARD:, :128] = piece[:32]
        out_ref[owner, SHARD:, 128:] = piece[32:]


def turn_weight(w_ref, out_ref):
    eye = (iota((128, 128), 0) == iota((128, 128), 1)).astype(F32).astype(BF16)
    for part in range(7):
        out_ref[part * 128 : part * 128 + 128, :] = mm(eye, w_ref[part], NT).astype(BF16)


def order_weight(w_ref, out_ref):
    out_ref[...] = mm(w_ref[...], order_matrix(), NT).astype(BF16)


def shifted(value, by, keep):
    return jnp.where(keep, pltpu.roll(value, (-by) % IMG, 1), 0.0)


def fold(taps, sign, cols_ref):
    lane = iota((OWN, IMG), 1)
    col = jnp.broadcast_to(cols_ref[...], (OWN, IMG))
    keep_col = {1: col != COLS - 1, -1: col != 0}
    keep_row = {1: lane < IMG - COLS, -1: lane >= COLS}
    total = None
    for j in range(3):
        line = None
        for k in range(3):
            value = taps[(3 * j + k) * OWN : (3 * j + k + 1) * OWN, :]
            step = sign * (k - 1)
            if step:
                value = shifted(value, step, keep_col[step])
            line = value if line is None else line + value
        step = sign * (j - 1)
        if step:
            line = shifted(line, step * COLS, keep_row[step])
        total = line if total is None else total + line
    return total


def convolve(frames, weight, dims, forward, cols_ref, own_ref, other_ref):
    if forward:
        plan = [(2, [(0, 0), (1, 1)], other_ref, 0), (3, [(1, 0)], other_ref, 1),
                (0, [(0, 2)], own_ref, 0), (1, [(0, 1), (1, 2)], own_ref, 1)]
    else:
        plan = [(-2, [(0, 0)], other_ref, 0), (-1, [(0, 1), (1, 0)], other_ref, 1),
                (0, [(0, 2), (1, 1)], own_ref, 0), (1, [(1, 2)], own_ref, 1)]
    for _, terms, ref, slot in plan:
        taps = None
        for frame, time_tap in terms:
            term = mm(weight[time_tap * 288 : time_tap * 288 + 288, :], frames[frame], dims)
            taps = term if taps is None else taps + term
        ref[:, slot * IMG : slot * IMG + IMG] = fold(taps, 1 if forward else -1, cols_ref)


def frame_of(ref, frame):
    return ref[:, frame * PART : frame * PART + PART, :].reshape(IMG, CH)


def first_conv(h_ref, stats_ref, x_ref, w_ref, vec_ref, cols_ref, own_ref, other_ref, raw_ref, column_ref):
    stats = stats_ref[...]
    lane = iota((16, 128), 1)
    mean = jnp.sum(stats, axis=0, keepdims=True) * (1.0 / 16)
    off = stats - mean
    spread_sum = jnp.sum(jnp.where(lane < 32, off * off * (POS * 8.0), stats), axis=0, keepdims=True)
    row = iota((8, 128), 0)
    lane8 = iota((8, 128), 1)
    both = jnp.where(row == 0, jnp.where(lane8 < 32, mean, 0.0), jnp.where(lane8 < 64, spread_sum, 0.0))
    expand = ((iota((128, CH), 0) & 31) == (iota((128, CH), 1) >> 3)).astype(F32)
    wide = exact(both, expand, NN)
    mean_c = wide[0:1]
    inv_c = lax.rsqrt(wide[1:2] * (1.0 / COUNT) + EPS)
    gain, shift = vec_ref[0:1], vec_ref[1:2]
    own = own_matrix(h_ref[0])
    row8 = iota((8, CH), 0)
    vectors = jnp.where(row8 == 4, mean_c, jnp.where(row8 == 5, inv_c, vec_ref[...]))
    columns = exact(own, vectors, NT)
    column_ref[...] = columns
    own16 = own.astype(BF16)
    acts = []
    for frame in range(2):
        raw = frame_of(x_ref, frame)
        raw_ref[:, frame * IMG : frame * IMG + IMG] = mm(own16, raw, NT).astype(BF16)
        pre = (raw.astype(F32) - mean_c) * inv_c * gain + shift
        acts.append((pre * jax.nn.sigmoid(pre)).astype(BF16))
    convolve(acts, w_ref, NT, True, cols_ref, own_ref, other_ref)


def lanes_of(values):
    lane = iota((1, 128), 1)
    row = jnp.zeros((1, 128), F32)
    for n, value in enumerate(values):
        row = jnp.where(lane == n, value, row)
    return row


def lane_of(row, n):
    return jnp.sum(jnp.where(iota((1, 128), 1) == n, row, 0.0), axis=1, keepdims=True)


def total_of(value):
    return jnp.sum(jnp.sum(value, axis=1, keepdims=True), axis=0, keepdims=True)


def hidden_stats(own_ref, got_ref, raw_ref, pack_ref, row_ref):
    hidden = (own_ref[...] + got_ref[...]).astype(BF16)
    pack_ref[:OWN, :] = hidden
    pack_ref[OWN:, :] = raw_ref[...]
    means, spreads = [], []
    for g in range(4):
        value = hidden.astype(F32)[8 * g : 8 * g + 8]
        mean = total_of(value) * (1.0 / (8 * POS))
        off = value - mean
        means.append(mean)
        spreads.append(total_of(off * off))
    row_ref[...] = lanes_of(means + spreads)


def silu_slope(value):
    sigma = jax.nn.sigmoid(value)
    return sigma * (1.0 + value * (1.0 - sigma))


def second_conv(h_ref, g_ref, w_ref, cols_ref, own_ref, other_ref, grad_ref):
    own16 = own_matrix(h_ref[0]).astype(BF16)
    frames = [frame_of(g_ref, frame) for frame in range(2)]
    convolve(frames, w_ref, NT, False, cols_ref, own_ref, other_ref)
    for frame in range(2):
        grad_ref[:, frame * IMG : frame * IMG + IMG] = mm(own16, frames[frame], NT)


def second_slope(place_ref, stats_ref, pack_ref, before_ref, own_ref, other_ref, column_ref, factor_ref, normed_ref, inv_ref, row_ref):
    stats = stats_ref[...]
    mean_row = jnp.sum(stats, axis=0, keepdims=True) * (1.0 / 16)
    off = stats - mean_row
    between = jnp.sum(off * off, axis=0, keepdims=True) * (8.0 * POS)
    within = jnp.sum(stats, axis=0, keepdims=True)
    has_before = place_ref[1] > 0
    hidden = pack_ref[...].astype(F32)
    before = before_ref[...].astype(F32)
    firsts, seconds, invs = [], [], []
    for g in range(4):
        rows = slice(8 * g, 8 * g + 8)
        mean = lane_of(mean_row, g)
        inv = lax.rsqrt((lane_of(between, g) + lane_of(within, 4 + g)) * (1.0 / COUNT) + EPS)
        gain, shift = column_ref[rows, 2:3], column_ref[rows, 3:4]
        normed = (hidden[rows] - mean) * inv
        factor = silu_slope(normed * gain + shift) * gain
        factor_ref[rows, :] = factor
        normed_ref[rows, :] = normed
        slope = own_ref[rows, :] * factor
        normed_before = (before[rows] - mean) * inv
        slope_before = other_ref[rows, :] * (silu_slope(normed_before * gain + shift) * gain)
        slope_before = jnp.where(has_before, slope_before, 0.0)
        firsts.append(total_of(slope + slope_before))
        seconds.append(total_of(slope * normed + slope_before * normed_before))
        invs.append(inv)
    inv_ref[...] = lanes_of(invs)
    row_ref[...] = lanes_of(firsts + seconds)


def hidden_grad(sums_ref, own_ref, got_ref, factor_ref, normed_ref, inv_ref, out_ref):
    means = jnp.sum(sums_ref[...], axis=0, keepdims=True) * (1.0 / COUNT)
    values = []
    for g in range(4):
        rows = slice(8 * g, 8 * g + 8)
        inv = lane_of(inv_ref[...], g)
        slope = (own_ref[rows, :] + got_ref[rows, :]) * factor_ref[rows, :]
        values.append(inv * (slope - lane_of(means, g) - normed_ref[rows, :] * lane_of(means, 4 + g)))
    out_ref[...] = jnp.concatenate(values, axis=0).astype(BF16)


def third_conv(place_ref, g_ref, w_ref, cols_ref, pack_ref, before_ref, column_ref, own_ref, other_ref, factor_ref, normed_ref, row_ref):
    frames = [
        g_ref[:, :, frame * IMG : frame * IMG + IMG].reshape(CH, IMG) for frame in range(2)
    ]
    convolve(frames, w_ref, NN, False, cols_ref, own_ref, other_ref)
    gain, shift = column_ref[:, 0:1], column_ref[:, 1:2]
    mean, inv = column_ref[:, 4:5], column_ref[:, 5:6]
    normed = (pack_ref[OWN:, :].astype(F32) - mean) * inv
    factor = silu_slope(normed * gain + shift) * gain
    normed_before = (before_ref[OWN:, :].astype(F32) - mean) * inv
    factor_before = silu_slope(normed_before * gain + shift) * gain
    factor_ref[...] = factor
    normed_ref[...] = normed
    slope = own_ref[...] * factor
    slope_before = jnp.where(place_ref[1] > 0, other_ref[...] * factor_before, 0.0)
    first = slope + slope_before
    second = slope * normed + slope_before * normed_before
    row_ref[...] = lanes_of(
        [total_of(value[8 * g : 8 * g + 8]) for value in (first, second) for g in range(4)]
    )


def input_grad(sums_ref, own_ref, got_ref, factor_ref, normed_ref, column_ref, grad_ref, out_ref):
    means = jnp.sum(sums_ref[...], axis=0, keepdims=True) * (1.0 / COUNT)
    values = []
    for g in range(4):
        rows = slice(8 * g, 8 * g + 8)
        slope = (own_ref[rows, :] + got_ref[rows, :]) * factor_ref[rows, :]
        inner = slope - lane_of(means, g) - normed_ref[rows, :] * lane_of(means, 4 + g)
        values.append(grad_ref[rows, :] + column_ref[rows, 5:6] * inner)
    value = jnp.concatenate(values, axis=0)
    for frame in range(2):
        image = value[:, frame * IMG : frame * IMG + IMG]
        for owner in range(8):
            moved = pltpu.roll(image, (-owner * PART) % IMG, 1) if owner else image
            out_ref[owner, :, frame * 128 : frame * 128 + 128] = moved[:, :128].astype(BF16)


def gather_rows(got_ref, out_ref):
    order = order_matrix()
    for frame in range(2):
        value = got_ref[:, :, frame * 128 : frame * 128 + 128].reshape(CH, 128)
        out_ref[frame * PART : frame * PART + PART, :] = mm(value, order, TN)[:PART].astype(BF16)


def on_device(inputs, grad_out, conv1_weight, conv2_weight, gain1, shift1, gain2, shift2):
    x = inputs.reshape(SHARD, CH)
    upstream = grad_out.reshape(SHARD, CH)
    place = jnp.stack([lax.axis_index("height"), lax.axis_index("tm")]).astype(jnp.int32)
    cols = jnp.asarray(np.arange(IMG)[None, :] % COLS, jnp.int32)
    zero = jnp.zeros_like(gain1)
    vectors = jnp.stack([gain1, shift1, gain2, shift2, zero, zero, zero, zero])
    half = shape(OWN, POS)
    row = shape(1, 128)

    taps = jnp.pad(conv1_weight.reshape(27, 8, CH), ((0, 5), (0, 0), (0, 0)))
    taps = taps.reshape(8, 4, 8, CH).transpose(1, 0, 2, 3).reshape(4, 64, CH)
    parcel = call(first_parcel, shape(8, SHARD + 32, CH, dtype=BF16), x, taps)
    x_all = lax.all_to_all(parcel, "height", 0, 0, tiled=True)
    stats1 = call(first_stats, row, x_all)
    stats1, pieces, second = lax.optimization_barrier(
        (stats1, x_all[:, SHARD:].reshape(CH, CH), conv2_weight.reshape(216, CH))
    )
    stats1 = spread(stats1, "tm", 16).reshape(16, 128)
    weights = lax.all_gather(jnp.concatenate([pieces, second]), "dp")
    pieces = weights[:, :CH].reshape(4, 8, 4, 8, 2, 128).transpose(4, 2, 0, 1, 3, 5).reshape(8, CH, 128)
    w1_forward = call(turn_weight, shape(896, CH, dtype=BF16), pieces)
    w2_back = weights[:, CH:].reshape(4, 27, 8, CH).transpose(1, 0, 2, 3).reshape(864, CH)

    own, other, raw, columns = call(
        first_conv, [half, half, shape(OWN, POS, dtype=BF16), shape(OWN, 8)], place, stats1, x_all, w1_forward, vectors, cols, smem=1
    )
    got = to_later(other)
    pack, stats2 = call(hidden_stats, [shape(2 * OWN, POS, dtype=BF16), row], own, got, raw)
    stats2, upstream = lax.optimization_barrier((stats2, upstream))
    before = to_later(pack)
    stats2 = spread(stats2, "tm", 16).reshape(16, 128)
    g_all = lax.all_gather(upstream, "height")
    own, other, grad_t = call(second_conv, [half, half, half], place, g_all, w2_back, cols, smem=1)
    factor2, normed2, inv2, sums2 = call(
        second_slope, [half, half, row, row], place, stats2, pack, before, own, other, columns, smem=1
    )
    sums2, other, third = lax.optimization_barrier((sums2, other, conv1_weight.reshape(216, CH)))
    got = to_earlier(other)
    sums2 = spread(sums2, "tm", 16).reshape(16, 128)
    third = lax.all_gather(third, "dp").reshape(4, 27, 8, CH).transpose(1, 0, 2, 3).reshape(864, CH)
    w1_back = call(order_weight, shape(864, CH, dtype=BF16), third)
    grad_hidden = call(hidden_grad, shape(OWN, POS, dtype=BF16), sums2, own, got, factor2, normed2, inv2)
    grad_hidden = lax.all_gather(grad_hidden, "height")
    own, other, factor1, normed1, sums1 = call(
        third_conv, [half, half, half, half, row], place, grad_hidden, w1_back, cols, pack, before, columns, smem=1
    )
    got = to_earlier(other)
    sums1 = spread(sums1, "tm", 16).reshape(16, 128)
    result = call(
        input_grad, shape(8, OWN, 256, dtype=BF16), sums1, own, got, factor1, normed1, columns, grad_t
    )
    result = lax.all_to_all(result, "height", 0, 0, tiled=True)
    return call(gather_rows, shape(SHARD, CH, dtype=BF16), result).reshape(inputs.shape)


def solution(mesh):
    return jax.shard_map(
        on_device,
        mesh=mesh,
        in_specs=(
            P("dp", "tm", "height", None, None),
            P("dp", "tm", "height", None, None),
            P(None, None, ("dp", "height"), None),
            P(None, None, ("dp", "height"), None),
            P(),
            P(),
            P(),
            P(),
        ),
        out_specs=P("dp", "tm", "height", None, None),
        check_vma=False,
    )
```

```python
import jax
import jax.numpy as jnp
import numpy as np
from jax import lax
from jax.experimental import pallas as pl
from jax.experimental.pallas import tpu as pltpu
from jax.sharding import PartitionSpec as P

EPS = 1e-06
F32 = jnp.float32
BF16 = jnp.bfloat16
CH = 256
OWN = 32
COLS = 40
IMG = 640
POS = 2 * IMG
SHARD = 160
PART = 80
COUNT = 32 * IMG * 8


def iota(shape, dim):
    return lax.broadcasted_iota(jnp.int32, shape, dim)


def exact(a, b, dims):
    return lax.dot_general(
        a, b, (dims, ((), ())), precision=lax.Precision.HIGHEST, preferred_element_type=F32
    )


def mm(a, b, dims):
    return lax.dot_general(a, b, (dims, ((), ())), preferred_element_type=F32)


NT = ((1,), (1,))
NN = ((1,), (0,))
TN = ((0,), (0,))


def channel_of(index):
    return ((index >> 3) & 3) * 64 + (index >> 5) * 8 + (index & 7)


def order_matrix():
    return (iota((CH, CH), 1) == channel_of(iota((CH, CH), 0))).astype(F32).astype(BF16)


def own_matrix(h):
    place = iota((OWN, CH), 0)
    return (iota((OWN, CH), 1) == (place >> 3) * 64 + h * 8 + (place & 7)).astype(F32)


def call(kernel, outs, *args, smem=0, flops=10**7):
    many = isinstance(outs, (list, tuple))
    specs = [pl.BlockSpec(memory_space=pltpu.SMEM)] * smem
    specs += [pl.BlockSpec(memory_space=pltpu.VMEM)] * (len(args) - smem)
    vmem = pl.BlockSpec(memory_space=pltpu.VMEM)
    return pl.pallas_call(
        kernel,
        out_shape=outs,
        in_specs=specs,
        out_specs=[vmem] * len(outs) if many else vmem,
        compiler_params=pltpu.CompilerParams(vmem_limit_bytes=32 * 2**20),
        cost_estimate=pl.CostEstimate(flops=flops, bytes_accessed=10**6, transcendentals=0),
    )(*args)


def shape(*dims, dtype=F32):
    return jax.ShapeDtypeStruct(dims, dtype)


def spread(block, axis, count):
    return lax.all_to_all(
        jnp.broadcast_to(block[None], (count,) + block.shape), axis, 0, 0, tiled=True
    )


def to_later(block):
    size = lax.axis_size("tm")
    return lax.ppermute(block, "tm", [(i, i + 1) for i in range(size - 1)])


def to_earlier(block):
    size = lax.axis_size("tm")
    return lax.ppermute(block, "tm", [(i + 1, i) for i in range(size - 1)])


def first_stats(x_ref, row_ref):
    frames = [frame_of(x_ref, frame).astype(F32) for frame in range(2)]
    same = ((iota((CH, CH), 0) >> 3) == (iota((CH, CH), 1) >> 3)).astype(F32)
    group = iota((CH, 128), 0) >> 3
    lane = iota((CH, 128), 1)
    sums = sum(jnp.sum(x, axis=0, keepdims=True) for x in frames)
    mean = exact(jnp.broadcast_to(sums, (8, CH)), same, NN)[:1] * (1.0 / (POS * 8))
    squares = sum(jnp.sum((x - mean) * (x - mean), axis=0, keepdims=True) for x in frames)
    means = exact(
        jnp.broadcast_to(mean, (8, CH)), ((group == lane) & ((iota((CH, 128), 0) & 7) == 0)).astype(F32), NN
    )
    spreads = exact(jnp.broadcast_to(squares, (8, CH)), (group + 32 == lane).astype(F32), NN)
    row_ref[...] = (means + spreads)[:1]


def first_parcel(x_ref, w_ref, out_ref):
    total = None
    lane = iota((CH, 1024), 1)
    channel = ((lane >> 3) & 3) * 64 + (lane >> 7) * 8 + (lane & 7)
    hit = iota((CH, 1024), 0) == channel
    for a in range(4):
        place = (hit & (((lane >> 5) & 3) == a)).astype(F32).astype(BF16)
        term = mm(w_ref[a], place, NN)
        total = term if total is None else total + term
    for owner in range(8):
        piece = total[:, owner * 128 : owner * 128 + 128].astype(BF16)
        out_ref[owner, :SHARD, :] = x_ref[...]
        out_ref[owner, SHARD:, :128] = piece[:32]
        out_ref[owner, SHARD:, 128:] = piece[32:]


def turn_weight(w_ref, out_ref):
    eye = (iota((128, 128), 0) == iota((128, 128), 1)).astype(F32).astype(BF16)
    for part in range(7):
        out_ref[part * 128 : part * 128 + 128, :] = mm(eye, w_ref[part], NT).astype(BF16)


def order_weight(w_ref, out_ref):
    out_ref[...] = mm(w_ref[...], order_matrix(), NT).astype(BF16)


def shifted(value, by, keep):
    return jnp.where(keep, pltpu.roll(value, (-by) % IMG, 1), 0.0)


def fold(taps, sign, cols_ref):
    lane = iota((OWN, IMG), 1)
    col = jnp.broadcast_to(cols_ref[...], (OWN, IMG))
    keep_col = {1: col != COLS - 1, -1: col != 0}
    keep_row = {1: lane < IMG - COLS, -1: lane >= COLS}
    total = None
    for j in range(3):
        line = None
        for k in range(3):
            value = taps[(3 * j + k) * OWN : (3 * j + k + 1) * OWN, :]
            step = sign * (k - 1)
            if step:
                value = shifted(value, step, keep_col[step])
            line = value if line is None else line + value
        step = sign * (j - 1)
        if step:
            line = shifted(line, step * COLS, keep_row[step])
        total = line if total is None else total + line
    return total


def convolve(frames, weight, dims, forward, cols_ref, own_ref, other_ref):
    if forward:
        plan = [(2, [(0, 0), (1, 1)], other_ref, 0), (3, [(1, 0)], other_ref, 1),
                (0, [(0, 2)], own_ref, 0), (1, [(0, 1), (1, 2)], own_ref, 1)]
    else:
        plan = [(-2, [(0, 0)], other_ref, 0), (-1, [(0, 1), (1, 0)], other_ref, 1),
                (0, [(0, 2), (1, 1)], own_ref, 0), (1, [(1, 2)], own_ref, 1)]
    for _, terms, ref, slot in plan:
        taps = None
        for frame, time_tap in terms:
            term = mm(weight[time_tap * 288 : time_tap * 288 + 288, :], frames[frame], dims)
            taps = term if taps is None else taps + term
        ref[:, slot * IMG : slot * IMG + IMG] = fold(taps, 1 if forward else -1, cols_ref)


def frame_of(ref, frame):
    return ref[:, frame * PART : frame * PART + PART, :].reshape(IMG, CH)


def first_conv(h_ref, stats_ref, x_ref, w_ref, vec_ref, cols_ref, own_ref, other_ref, raw_ref, column_ref):
    stats = stats_ref[...]
    lane = iota((16, 128), 1)
    mean = jnp.sum(stats, axis=0, keepdims=True) * (1.0 / 16)
    off = stats - mean
    spread_sum = jnp.sum(jnp.where(lane < 32, off * off * (POS * 8.0), stats), axis=0, keepdims=True)
    row = iota((8, 128), 0)
    lane8 = iota((8, 128), 1)
    both = jnp.where(row == 0, jnp.where(lane8 < 32, mean, 0.0), jnp.where(lane8 < 64, spread_sum, 0.0))
    expand = ((iota((128, CH), 0) & 31) == (iota((128, CH), 1) >> 3)).astype(F32)
    wide = exact(both, expand, NN)
    mean_c = wide[0:1]
    inv_c = lax.rsqrt(wide[1:2] * (1.0 / COUNT) + EPS)
    gain, shift = vec_ref[0:1], vec_ref[1:2]
    own = own_matrix(h_ref[0])
    row8 = iota((8, CH), 0)
    vectors = jnp.where(row8 == 4, mean_c, jnp.where(row8 == 5, inv_c, vec_ref[...]))
    columns = exact(own, vectors, NT)
    column_ref[...] = columns
    own16 = own.astype(BF16)
    acts = []
    for frame in range(2):
        raw = frame_of(x_ref, frame)
        raw_ref[:, frame * IMG : frame * IMG + IMG] = mm(own16, raw, NT).astype(BF16)
        pre = (raw.astype(F32) - mean_c) * inv_c * gain + shift
        acts.append((pre * jax.nn.sigmoid(pre)).astype(BF16))
    convolve(acts, w_ref, NT, True, cols_ref, own_ref, other_ref)


def lanes_of(values):
    lane = iota((1, 128), 1)
    row = jnp.zeros((1, 128), F32)
    for n, value in enumerate(values):
        row = jnp.where(lane == n, value, row)
    return row


def lane_of(row, n):
    return jnp.sum(jnp.where(iota((1, 128), 1) == n, row, 0.0), axis=1, keepdims=True)


def total_of(value):
    return jnp.sum(jnp.sum(value, axis=1, keepdims=True), axis=0, keepdims=True)


def hidden_stats(own_ref, got_ref, raw_ref, pack_ref, row_ref):
    hidden = (own_ref[...] + got_ref[...]).astype(BF16)
    pack_ref[:OWN, :] = hidden
    pack_ref[OWN:, :] = raw_ref[...]
    means, spreads = [], []
    for g in range(4):
        value = hidden.astype(F32)[8 * g : 8 * g + 8]
        mean = total_of(value) * (1.0 / (8 * POS))
        off = value - mean
        means.append(mean)
        spreads.append(total_of(off * off))
    row_ref[...] = lanes_of(means + spreads)


def silu_slope(value):
    sigma = jax.nn.sigmoid(value)
    return sigma * (1.0 + value * (1.0 - sigma))


def second_conv(h_ref, g_ref, w_ref, cols_ref, own_ref, other_ref, grad_ref):
    own16 = own_matrix(h_ref[0]).astype(BF16)
    frames = [frame_of(g_ref, frame) for frame in range(2)]
    convolve(frames, w_ref, NT, False, cols_ref, own_ref, other_ref)
    for frame in range(2):
        grad_ref[:, frame * IMG : frame * IMG + IMG] = mm(own16, frames[frame], NT)


def second_slope(place_ref, stats_ref, pack_ref, before_ref, own_ref, other_ref, column_ref, factor_ref, normed_ref, inv_ref, row_ref):
    stats = stats_ref[...]
    mean_row = jnp.sum(stats, axis=0, keepdims=True) * (1.0 / 16)
    off = stats - mean_row
    between = jnp.sum(off * off, axis=0, keepdims=True) * (8.0 * POS)
    within = jnp.sum(stats, axis=0, keepdims=True)
    has_before = place_ref[1] > 0
    hidden = pack_ref[...].astype(F32)
    before = before_ref[...].astype(F32)
    firsts, seconds, invs = [], [], []
    for g in range(4):
        rows = slice(8 * g, 8 * g + 8)
        mean = lane_of(mean_row, g)
        inv = lax.rsqrt((lane_of(between, g) + lane_of(within, 4 + g)) * (1.0 / COUNT) + EPS)
        gain, shift = column_ref[rows, 2:3], column_ref[rows, 3:4]
        normed = (hidden[rows] - mean) * inv
        factor = silu_slope(normed * gain + shift) * gain
        factor_ref[rows, :] = factor
        normed_ref[rows, :] = normed
        slope = own_ref[rows, :] * factor
        normed_before = (before[rows] - mean) * inv
        slope_before = other_ref[rows, :] * (silu_slope(normed_before * gain + shift) * gain)
        slope_before = jnp.where(has_before, slope_before, 0.0)
        firsts.append(total_of(slope + slope_before))
        seconds.append(total_of(slope * normed + slope_before * normed_before))
        invs.append(inv)
    inv_ref[...] = lanes_of(invs)
    row_ref[...] = lanes_of(firsts + seconds)


def hidden_grad(sums_ref, own_ref, got_ref, factor_ref, normed_ref, inv_ref, out_ref):
    means = jnp.sum(sums_ref[...], axis=0, keepdims=True) * (1.0 / COUNT)
    values = []
    for g in range(4):
        rows = slice(8 * g, 8 * g + 8)
        inv = lane_of(inv_ref[...], g)
        slope = (own_ref[rows, :] + got_ref[rows, :]) * factor_ref[rows, :]
        values.append(inv * (slope - lane_of(means, g) - normed_ref[rows, :] * lane_of(means, 4 + g)))
    out_ref[...] = jnp.concatenate(values, axis=0).astype(BF16)


def third_conv(place_ref, g_ref, w_ref, cols_ref, pack_ref, before_ref, column_ref, own_ref, other_ref, factor_ref, normed_ref, row_ref):
    frames = [
        g_ref[:, :, frame * IMG : frame * IMG + IMG].reshape(CH, IMG) for frame in range(2)
    ]
    convolve(frames, w_ref, NN, False, cols_ref, own_ref, other_ref)
    gain, shift = column_ref[:, 0:1], column_ref[:, 1:2]
    mean, inv = column_ref[:, 4:5], column_ref[:, 5:6]
    normed = (pack_ref[OWN:, :].astype(F32) - mean) * inv
    factor = silu_slope(normed * gain + shift) * gain
    normed_before = (before_ref[OWN:, :].astype(F32) - mean) * inv
    factor_before = silu_slope(normed_before * gain + shift) * gain
    factor_ref[...] = factor
    normed_ref[...] = normed
    slope = own_ref[...] * factor
    slope_before = jnp.where(place_ref[1] > 0, other_ref[...] * factor_before, 0.0)
    first = slope + slope_before
    second = slope * normed + slope_before * normed_before
    row_ref[...] = lanes_of(
        [total_of(value[8 * g : 8 * g + 8]) for value in (first, second) for g in range(4)]
    )


def border_slope(own_ref, got_ref, factor_ref, slope_ref):
    slope_ref[...] = (own_ref[...] + got_ref[...]) * factor_ref[...]


def input_grad(sums_ref, slope_ref, normed_ref, column_ref, grad_ref, out_ref):
    means = jnp.sum(sums_ref[...], axis=0, keepdims=True) * (1.0 / COUNT)
    values = []
    for g in range(4):
        rows = slice(8 * g, 8 * g + 8)
        inner = slope_ref[rows, :] - lane_of(means, g) - normed_ref[rows, :] * lane_of(means, 4 + g)
        values.append(grad_ref[rows, :] + column_ref[rows, 5:6] * inner)
    value = jnp.concatenate(values, axis=0)
    for frame in range(2):
        image = value[:, frame * IMG : frame * IMG + IMG]
        for owner in range(8):
            moved = pltpu.roll(image, (-owner * PART) % IMG, 1) if owner else image
            out_ref[owner, :, frame * 128 : frame * 128 + 128] = moved[:, :128].astype(BF16)


def gather_rows(got_ref, out_ref):
    order = order_matrix()
    for frame in range(2):
        value = got_ref[:, :, frame * 128 : frame * 128 + 128].reshape(CH, 128)
        out_ref[frame * PART : frame * PART + PART, :] = mm(value, order, TN)[:PART].astype(BF16)


def on_device(inputs, grad_out, conv1_weight, conv2_weight, gain1, shift1, gain2, shift2):
    x = inputs.reshape(SHARD, CH)
    upstream = grad_out.reshape(SHARD, CH)
    place = jnp.stack([lax.axis_index("height"), lax.axis_index("tm")]).astype(jnp.int32)
    cols = jnp.asarray(np.arange(IMG)[None, :] % COLS, jnp.int32)
    zero = jnp.zeros_like(gain1)
    vectors = jnp.stack([gain1, shift1, gain2, shift2, zero, zero, zero, zero])
    half = shape(OWN, POS)
    row = shape(1, 128)

    both = jnp.concatenate([conv2_weight.reshape(216, CH), conv1_weight.reshape(216, CH)])
    both = lax.all_gather(jnp.pad(both, ((0, 144), (0, 0))), "dp")
    w2_back, third = (
        both[:, n * 216 : n * 216 + 216].reshape(4, 27, 8, CH).transpose(1, 0, 2, 3).reshape(864, CH)
        for n in range(2)
    )
    g_all = lax.all_gather(jnp.pad(upstream, ((0, 128), (0, 0))), "height")
    taps = jnp.pad(conv1_weight.reshape(27, 8, CH), ((0, 5), (0, 0), (0, 0)))
    taps = taps.reshape(8, 4, 8, CH).transpose(1, 0, 2, 3).reshape(4, 64, CH)
    parcel = call(first_parcel, shape(8, SHARD + 32, CH, dtype=BF16), x, taps)
    x_all = lax.all_to_all(parcel, "height", 0, 0, tiled=True)
    stats1 = call(first_stats, row, x_all)
    stats1, pieces = lax.optimization_barrier((stats1, x_all[:, SHARD:].reshape(CH, CH)))
    stats1 = spread(stats1, "tm", 16).reshape(16, 128)
    pieces = lax.all_gather(pieces, "dp").reshape(4, 8, 4, 8, 2, 128).transpose(4, 2, 0, 1, 3, 5).reshape(8, CH, 128)
    w1_forward = call(turn_weight, shape(896, CH, dtype=BF16), pieces)

    own, other, raw, columns = call(
        first_conv, [half, half, shape(OWN, POS, dtype=BF16), shape(OWN, 8)], place, stats1, x_all, w1_forward, vectors, cols, smem=1
    )
    got = to_later(other)
    pack, stats2 = call(hidden_stats, [shape(2 * OWN, POS, dtype=BF16), row], own, got, raw)
    before = to_later(pack)
    stats2 = spread(stats2, "tm", 16).reshape(16, 128)
    own, other, grad_t = call(second_conv, [half, half, half], place, g_all, w2_back, cols, smem=1)
    factor2, normed2, inv2, sums2 = call(
        second_slope, [half, half, row, row], place, stats2, pack, before, own, other, columns, smem=1
    )
    sums2, other = lax.optimization_barrier((sums2, other))
    got = to_earlier(other)
    sums2 = spread(sums2, "tm", 16).reshape(16, 128)
    w1_back = call(order_weight, shape(864, CH, dtype=BF16), third)
    grad_hidden = call(hidden_grad, shape(OWN, POS, dtype=BF16), sums2, own, got, factor2, normed2, inv2)
    grad_hidden = lax.all_gather(grad_hidden, "height")
    own, other, factor1, normed1, sums1 = call(
        third_conv, [half, half, half, half, row], place, grad_hidden, w1_back, cols, pack, before, columns, smem=1
    )
    slope1 = call(border_slope, half, own, to_earlier(other), factor1, flops=3 * 10**10)
    sums1 = spread(sums1, "tm", 16).reshape(16, 128)
    result = call(
        input_grad, shape(8, OWN, 256, dtype=BF16), sums1, slope1, normed1, columns, grad_t
    )
    result = lax.all_to_all(result, "height", 0, 0, tiled=True)
    return call(gather_rows, shape(SHARD, CH, dtype=BF16), result).reshape(inputs.shape)


def solution(mesh):
    return jax.shard_map(
        on_device,
        mesh=mesh,
        in_specs=(
            P("dp", "tm", "height", None, None),
            P("dp", "tm", "height", None, None),
            P(None, None, ("dp", "height"), None),
            P(None, None, ("dp", "height"), None),
            P(),
            P(),
            P(),
            P(),
        ),
        out_specs=P("dp", "tm", "height", None, None),
        check_vma=False,
    )
```

```python
import jax
import jax.numpy as jnp
import numpy as np
from jax import lax
from jax.experimental import pallas as pl
from jax.experimental.pallas import tpu as pltpu
from jax.sharding import PartitionSpec as P

EPS = 1e-06
F32 = jnp.float32
BF16 = jnp.bfloat16
CH = 256
OWN = 32
COLS = 40
IMG = 640
POS = 2 * IMG
SHARD = 160
PART = 80
COUNT = 32 * IMG * 8


def iota(shape, dim):
    return lax.broadcasted_iota(jnp.int32, shape, dim)


def exact(a, b, dims):
    return lax.dot_general(
        a, b, (dims, ((), ())), precision=lax.Precision.HIGHEST, preferred_element_type=F32
    )


def mm(a, b, dims):
    return lax.dot_general(a, b, (dims, ((), ())), preferred_element_type=F32)


NT = ((1,), (1,))
NN = ((1,), (0,))
TN = ((0,), (0,))


def channel_of(index):
    return ((index >> 3) & 3) * 64 + (index >> 5) * 8 + (index & 7)


def order_matrix():
    return (iota((CH, CH), 1) == channel_of(iota((CH, CH), 0))).astype(F32).astype(BF16)


def own_matrix(h):
    place = iota((OWN, CH), 0)
    return (iota((OWN, CH), 1) == (place >> 3) * 64 + h * 8 + (place & 7)).astype(F32)


def call(kernel, outs, *args, smem=0, flops=10**7):
    many = isinstance(outs, (list, tuple))
    specs = [pl.BlockSpec(memory_space=pltpu.SMEM)] * smem
    specs += [pl.BlockSpec(memory_space=pltpu.VMEM)] * (len(args) - smem)
    vmem = pl.BlockSpec(memory_space=pltpu.VMEM)
    return pl.pallas_call(
        kernel,
        out_shape=outs,
        in_specs=specs,
        out_specs=[vmem] * len(outs) if many else vmem,
        compiler_params=pltpu.CompilerParams(vmem_limit_bytes=32 * 2**20),
        cost_estimate=pl.CostEstimate(flops=flops, bytes_accessed=10**6, transcendentals=0),
    )(*args)


def shape(*dims, dtype=F32):
    return jax.ShapeDtypeStruct(dims, dtype)


def spread(block, axis, count):
    return lax.all_to_all(
        jnp.broadcast_to(block[None], (count,) + block.shape), axis, 0, 0, tiled=True
    )


def to_later(block):
    size = lax.axis_size("tm")
    return lax.ppermute(block, "tm", [(i, i + 1) for i in range(size - 1)])


def to_earlier(block):
    size = lax.axis_size("tm")
    return lax.ppermute(block, "tm", [(i + 1, i) for i in range(size - 1)])


def by_tap(weight):
    return weight.reshape(4, 27, 8, CH).transpose(1, 0, 2, 3).reshape(864, CH)


def opening(x_ref, w_ref, out_ref, row_ref):
    x = x_ref[...].astype(F32)
    same = ((iota((CH, CH), 0) >> 3) == (iota((CH, CH), 1) >> 3)).astype(F32)
    group = iota((CH, 128), 0) >> 3
    lane = iota((CH, 128), 1)
    sums = jnp.sum(x, axis=0, keepdims=True)
    mean = exact(jnp.broadcast_to(sums, (8, CH)), same, NN)[:1] * (1.0 / (SHARD * 8))
    squares = jnp.sum((x - mean) * (x - mean), axis=0, keepdims=True)
    means = exact(
        jnp.broadcast_to(mean, (8, CH)), ((group == lane) & ((iota((CH, 128), 0) & 7) == 0)).astype(F32), NN
    )
    spreads = exact(jnp.broadcast_to(squares, (8, CH)), (group + 32 == lane).astype(F32), NN)
    row_ref[...] = (means + spreads)[:1]
    total = None
    lane = iota((CH, 1024), 1)
    channel = ((lane >> 3) & 3) * 64 + (lane >> 7) * 8 + (lane & 7)
    hit = iota((CH, 1024), 0) == channel
    for a in range(4):
        place = (hit & (((lane >> 5) & 3) == a)).astype(F32).astype(BF16)
        term = mm(w_ref[a], place, NN)
        total = term if total is None else total + term
    for owner in range(8):
        piece = total[:, owner * 128 : owner * 128 + 128].astype(BF16)
        out_ref[owner, :, :128] = piece[:32]
        out_ref[owner, :, 128:] = piece[32:]


def turn_weight(w_ref, out_ref):
    eye = (iota((128, 128), 0) == iota((128, 128), 1)).astype(F32).astype(BF16)
    for part in range(7):
        out_ref[part * 128 : part * 128 + 128, :] = mm(eye, w_ref[part], NT).astype(BF16)


def order_weight(w_ref, out_ref):
    out_ref[...] = mm(w_ref[...], order_matrix(), NT).astype(BF16)


def shifted(value, by, keep):
    return jnp.where(keep, pltpu.roll(value, (-by) % IMG, 1), 0.0)


def fold(taps, sign, cols_ref):
    lane = iota((OWN, IMG), 1)
    col = jnp.broadcast_to(cols_ref[...], (OWN, IMG))
    keep_col = {1: col != COLS - 1, -1: col != 0}
    keep_row = {1: lane < IMG - COLS, -1: lane >= COLS}
    total = None
    for j in range(3):
        line = None
        for k in range(3):
            value = taps[(3 * j + k) * OWN : (3 * j + k + 1) * OWN, :]
            step = sign * (k - 1)
            if step:
                value = shifted(value, step, keep_col[step])
            line = value if line is None else line + value
        step = sign * (j - 1)
        if step:
            line = shifted(line, step * COLS, keep_row[step])
        total = line if total is None else total + line
    return total


def convolve(frames, weight, dims, forward, cols_ref, own_ref, other_ref):
    if forward:
        plan = [(2, [(0, 0), (1, 1)], other_ref, 0), (3, [(1, 0)], other_ref, 1),
                (0, [(0, 2)], own_ref, 0), (1, [(0, 1), (1, 2)], own_ref, 1)]
    else:
        plan = [(-2, [(0, 0)], other_ref, 0), (-1, [(0, 1), (1, 0)], other_ref, 1),
                (0, [(0, 2), (1, 1)], own_ref, 0), (1, [(1, 2)], own_ref, 1)]
    for _, terms, ref, slot in plan:
        taps = None
        for frame, time_tap in terms:
            term = mm(weight[time_tap * 288 : time_tap * 288 + 288, :], frames[frame], dims)
            taps = term if taps is None else taps + term
        ref[:, slot * IMG : slot * IMG + IMG] = fold(taps, 1 if forward else -1, cols_ref)


def frame_of(ref, frame, base):
    start = base + frame * PART
    return ref[:, start : start + PART, :].reshape(IMG, CH)


def first_conv(h_ref, stats_ref, x_ref, w_ref, vec_ref, cols_ref, own_ref, other_ref, raw_ref, column_ref):
    stats = stats_ref[...]
    lane = iota((128, 128), 1)
    mean = jnp.sum(stats, axis=0, keepdims=True) * (1.0 / 128)
    off = stats - mean
    spread_sum = jnp.sum(jnp.where(lane < 32, off * off * (SHARD * 8.0), stats), axis=0, keepdims=True)
    row = iota((8, 128), 0)
    lane8 = iota((8, 128), 1)
    both = jnp.where(row == 0, jnp.where(lane8 < 32, mean, 0.0), jnp.where(lane8 < 64, spread_sum, 0.0))
    expand = ((iota((128, CH), 0) & 31) == (iota((128, CH), 1) >> 3)).astype(F32)
    wide = exact(both, expand, NN)
    mean_c = wide[0:1]
    inv_c = lax.rsqrt(wide[1:2] * (1.0 / COUNT) + EPS)
    gain, shift = vec_ref[0:1], vec_ref[1:2]
    own = own_matrix(h_ref[0])
    row8 = iota((8, CH), 0)
    vectors = jnp.where(row8 == 4, mean_c, jnp.where(row8 == 5, inv_c, vec_ref[...]))
    columns = exact(own, vectors, NT)
    column_ref[...] = columns
    own16 = own.astype(BF16)
    acts = []
    for frame in range(2):
        raw = frame_of(x_ref, frame, 0)
        raw_ref[:, frame * IMG : frame * IMG + IMG] = mm(own16, raw, NT).astype(BF16)
        pre = (raw.astype(F32) - mean_c) * inv_c * gain + shift
        acts.append((pre * jax.nn.sigmoid(pre)).astype(BF16))
    convolve(acts, w_ref, NT, True, cols_ref, own_ref, other_ref)


def lanes_of(values):
    lane = iota((1, 128), 1)
    row = jnp.zeros((1, 128), F32)
    for n, value in enumerate(values):
        row = jnp.where(lane == n, value, row)
    return row


def lane_of(row, n):
    return jnp.sum(jnp.where(iota((1, 128), 1) == n, row, 0.0), axis=1, keepdims=True)


def total_of(value):
    return jnp.sum(jnp.sum(value, axis=1, keepdims=True), axis=0, keepdims=True)


def hidden_stats(own_ref, got_ref, hidden_ref, row_ref):
    hidden = (own_ref[...] + got_ref[...]).astype(BF16)
    hidden_ref[...] = hidden
    means, spreads = [], []
    for g in range(4):
        value = hidden.astype(F32)[8 * g : 8 * g + 8]
        mean = total_of(value) * (1.0 / (8 * POS))
        off = value - mean
        means.append(mean)
        spreads.append(total_of(off * off))
    row_ref[...] = lanes_of(means + spreads)


def silu_slope(value):
    sigma = jax.nn.sigmoid(value)
    return sigma * (1.0 + value * (1.0 - sigma))


def second_conv(h_ref, g_ref, w_ref, cols_ref, own_ref, other_ref, grad_ref):
    own16 = own_matrix(h_ref[0]).astype(BF16)
    frames = [frame_of(g_ref, frame, SHARD) for frame in range(2)]
    convolve(frames, w_ref, NT, False, cols_ref, own_ref, other_ref)
    for frame in range(2):
        grad_ref[:, frame * IMG : frame * IMG + IMG] = mm(own16, frames[frame], NT)


def second_slope(stats_ref, hidden_ref, own_ref, got_ref, column_ref, pack_ref, row_ref):
    stats = stats_ref[...]
    mean_row = jnp.sum(stats, axis=0, keepdims=True) * (1.0 / 16)
    off = stats - mean_row
    between = jnp.sum(off * off, axis=0, keepdims=True) * (8.0 * POS)
    within = jnp.sum(stats, axis=0, keepdims=True)
    hidden = hidden_ref[...].astype(F32)
    firsts, seconds, means, invs, slopes = [], [], [], [], []
    for g in range(4):
        rows = slice(8 * g, 8 * g + 8)
        mean = lane_of(mean_row, g)
        inv = lax.rsqrt((lane_of(between, g) + lane_of(within, 4 + g)) * (1.0 / COUNT) + EPS)
        gain, shift = column_ref[rows, 2:3], column_ref[rows, 3:4]
        normed = (hidden[rows] - mean) * inv
        slope = (own_ref[rows, :] + got_ref[rows, :]) * silu_slope(normed * gain + shift) * gain
        first = total_of(slope)
        slopes.append(slope - first * (1.0 / (8 * POS)))
        firsts.append(first)
        seconds.append(total_of(slope * normed))
        means.append(mean)
        invs.append(inv)
    pack_ref[:OWN, :] = jnp.concatenate(slopes, axis=0).astype(BF16)
    pack_ref[OWN:, :] = hidden_ref[...]
    row_ref[...] = lanes_of(firsts + seconds + means + invs)


def third_conv(place_ref, sums_ref, g_ref, w_ref, cols_ref, raw_ref, before_ref, column_ref, own_ref, other_ref, factor_ref, normed_ref, row_ref):
    sums = sums_ref[...].reshape(16, 8, 128)
    mine = jnp.sum(jnp.where(iota((16, 8, 128), 0) == place_ref[1], sums, 0.0), axis=0)
    total = jnp.sum(sums, axis=0)
    spread_rows = ((iota((CH, 8), 0) >> 5) == iota((CH, 8), 1)).astype(F32)
    quarter = (iota((CH, 128), 0) >> 3) & 3
    lane = iota((CH, 128), 1)

    def column(wide, first):
        return jnp.sum(jnp.where(lane == quarter + first, wide, 0.0), axis=1, keepdims=True)

    mine, total = exact(spread_rows, mine, NN), exact(spread_rows, total, NN)
    offset = column(mine, 0) * (1.0 / (8 * POS)) - column(total, 0) * (1.0 / COUNT)
    second = column(total, 4) * (1.0 / COUNT)
    mean, inv = column(mine, 8), column(mine, 12)
    frames = []
    for frame in range(2):
        lanes = slice(frame * IMG, frame * IMG + IMG)
        slope = g_ref[:, :OWN, lanes].reshape(CH, IMG).astype(F32) + offset
        normed = (g_ref[:, OWN:, lanes].reshape(CH, IMG).astype(F32) - mean) * inv
        frames.append((inv * (slope - normed * second)).astype(BF16))
    convolve(frames, w_ref, NN, False, cols_ref, own_ref, other_ref)
    gain, shift = column_ref[:, 0:1], column_ref[:, 1:2]
    mean, inv = column_ref[:, 4:5], column_ref[:, 5:6]
    normed = (raw_ref[...].astype(F32) - mean) * inv
    factor = silu_slope(normed * gain + shift) * gain
    normed_before = (before_ref[...].astype(F32) - mean) * inv
    factor_before = silu_slope(normed_before * gain + shift) * gain
    factor_ref[...] = factor
    normed_ref[...] = normed
    slope = own_ref[...] * factor
    slope_before = jnp.where(place_ref[1] > 0, other_ref[...] * factor_before, 0.0)
    first = slope + slope_before
    second = slope * normed + slope_before * normed_before
    row_ref[...] = lanes_of(
        [total_of(value[8 * g : 8 * g + 8]) for value in (first, second) for g in range(4)]
    )


def border_slope(own_ref, got_ref, factor_ref, slope_ref):
    slope_ref[...] = (own_ref[...] + got_ref[...]) * factor_ref[...]


def input_grad(sums_ref, slope_ref, normed_ref, column_ref, grad_ref, out_ref):
    means = jnp.sum(sums_ref[...], axis=0, keepdims=True) * (1.0 / COUNT)
    values = []
    for g in range(4):
        rows = slice(8 * g, 8 * g + 8)
        inner = slope_ref[rows, :] - lane_of(means, g) - normed_ref[rows, :] * lane_of(means, 4 + g)
        values.append(grad_ref[rows, :] + column_ref[rows, 5:6] * inner)
    value = jnp.concatenate(values, axis=0)
    for frame in range(2):
        image = value[:, frame * IMG : frame * IMG + IMG]
        for owner in range(8):
            moved = pltpu.roll(image, (-owner * PART) % IMG, 1) if owner else image
            out_ref[owner, :, frame * 128 : frame * 128 + 128] = moved[:, :128].astype(BF16)


def gather_rows(got_ref, out_ref):
    order = order_matrix()
    for frame in range(2):
        value = got_ref[:, :, frame * 128 : frame * 128 + 128].reshape(CH, 128)
        out_ref[frame * PART : frame * PART + PART, :] = mm(value, order, TN)[:PART].astype(BF16)


def on_device(inputs, grad_out, conv1_weight, conv2_weight, gain1, shift1, gain2, shift2):
    x = inputs.reshape(SHARD, CH)
    upstream = grad_out.reshape(SHARD, CH)
    place = jnp.stack([lax.axis_index("height"), lax.axis_index("tm")]).astype(jnp.int32)
    cols = jnp.asarray(np.arange(IMG)[None, :] % COLS, jnp.int32)
    zero = jnp.zeros_like(gain1)
    vectors = jnp.stack([gain1, shift1, gain2, shift2, zero, zero, zero, zero])
    half = shape(OWN, POS)
    half16 = shape(OWN, POS, dtype=BF16)
    row = shape(1, 128)

    all_rows = lax.all_gather(jnp.concatenate([x, upstream]), "height")
    taps = jnp.pad(conv1_weight.reshape(27, 8, CH), ((0, 5), (0, 0), (0, 0)))
    taps = taps.reshape(8, 4, 8, CH).transpose(1, 0, 2, 3).reshape(4, 64, CH)
    pieces, stats1 = call(opening, [shape(8, 32, CH, dtype=BF16), row], x, taps)
    pieces = lax.all_to_all(pieces, "height", 0, 0, tiled=True).reshape(CH, CH)
    pieces, stats1, third = lax.optimization_barrier((pieces, stats1, conv1_weight.reshape(216, CH)))
    stats1 = spread(stats1, ("tm", "height"), 128).reshape(128, 128)
    weights = lax.all_gather(jnp.concatenate([pieces, conv2_weight.reshape(216, CH)]), "dp")
    pieces = weights[:, :CH].reshape(4, 8, 4, 8, 2, 128).transpose(4, 2, 0, 1, 3, 5).reshape(8, CH, 128)
    w1_forward = call(turn_weight, shape(896, CH, dtype=BF16), pieces)
    w2_back = by_tap(weights[:, CH:])
    own, other, raw, columns = call(
        first_conv, [half, half, half16, shape(OWN, 8)], place, stats1, all_rows, w1_forward, vectors, cols, smem=1
    )
    got = to_later(other)
    third = lax.all_gather(jnp.pad(third, ((0, 360), (0, 0))), "dp")[:, :216]
    w1_back = call(order_weight, shape(864, CH, dtype=BF16), by_tap(third))
    own2, other2, grad_t = call(second_conv, [half, half, half], place, all_rows, w2_back, cols, smem=1)
    hidden, stats2 = call(hidden_stats, [half16, row], own, got)
    stats2, other2 = lax.optimization_barrier((stats2, other2))
    got2 = to_earlier(other2)
    stats2 = spread(stats2, "tm", 16).reshape(16, 128)
    pack, sums2 = call(
        second_slope, [shape(2 * OWN, POS, dtype=BF16), row], stats2, hidden, own2, got2, columns
    )
    pack, sums2, raw = lax.optimization_barrier((pack, sums2, raw))
    pack = lax.all_gather(pack, "height")
    before = to_later(raw)
    sums2 = spread(sums2, ("tm", "height"), 128).reshape(128, 128)
    own, other, factor1, normed1, sums1 = call(
        third_conv, [half, half, half, half, row], place, sums2, pack, w1_back, cols, raw, before, columns, smem=1
    )
    slope1 = call(border_slope, half, own, to_earlier(other), factor1, flops=3 * 10**10)
    sums1 = spread(sums1, "tm", 16).reshape(16, 128)
    result = call(
        input_grad, shape(8, OWN, 256, dtype=BF16), sums1, slope1, normed1, columns, grad_t
    )
    result = lax.all_to_all(result, "height", 0, 0, tiled=True)
    return call(gather_rows, shape(SHARD, CH, dtype=BF16), result).reshape(inputs.shape)


def solution(mesh):
    return jax.shard_map(
        on_device,
        mesh=mesh,
        in_specs=(
            P("dp", "tm", "height", None, None),
            P("dp", "tm", "height", None, None),
            P(None, None, ("dp", "height"), None),
            P(None, None, ("dp", "height"), None),
            P(),
            P(),
            P(),
            P(),
        ),
        out_specs=P("dp", "tm", "height", None, None),
        check_vma=False,
    )
```

```python
import jax
import jax.numpy as jnp
import numpy as np
from jax import lax
from jax.experimental import pallas as pl
from jax.experimental.pallas import tpu as pltpu
from jax.sharding import PartitionSpec as P

EPS = 1e-06
F32 = jnp.float32
BF16 = jnp.bfloat16
CH = 256
OWN = 32
COLS = 40
IMG = 640
POS = 2 * IMG
SHARD = 160
PART = 80
COUNT = 32 * IMG * 8


def iota(shape, dim):
    return lax.broadcasted_iota(jnp.int32, shape, dim)


def exact(a, b, dims):
    return lax.dot_general(
        a, b, (dims, ((), ())), precision=lax.Precision.HIGHEST, preferred_element_type=F32
    )


def mm(a, b, dims):
    return lax.dot_general(a, b, (dims, ((), ())), preferred_element_type=F32)


NT = ((1,), (1,))
NN = ((1,), (0,))
TN = ((0,), (0,))


def channel_of(index):
    return ((index >> 3) & 3) * 64 + (index >> 5) * 8 + (index & 7)


def order_matrix():
    return (iota((CH, CH), 1) == channel_of(iota((CH, CH), 0))).astype(F32).astype(BF16)


def own_matrix(h):
    place = iota((OWN, CH), 0)
    return (iota((OWN, CH), 1) == (place >> 3) * 64 + h * 8 + (place & 7)).astype(F32)


def call(kernel, outs, *args, smem=0, vmem_mib=32, flops=10**7):
    many = isinstance(outs, (list, tuple))
    specs = [pl.BlockSpec(memory_space=pltpu.SMEM)] * smem
    specs += [pl.BlockSpec(memory_space=pltpu.VMEM)] * (len(args) - smem)
    vmem = pl.BlockSpec(memory_space=pltpu.VMEM)
    return pl.pallas_call(
        kernel,
        out_shape=outs,
        in_specs=specs,
        out_specs=[vmem] * len(outs) if many else vmem,
        compiler_params=pltpu.CompilerParams(vmem_limit_bytes=vmem_mib * 2**20),
        cost_estimate=pl.CostEstimate(flops=flops, bytes_accessed=10**6, transcendentals=0),
    )(*args)


def shape(*dims, dtype=F32):
    return jax.ShapeDtypeStruct(dims, dtype)


def exchanged(rows, axis):
    return lax.all_to_all(rows, axis, 0, 0, tiled=True).reshape(rows.shape[0], 128)


def to_later(block):
    size = lax.axis_size("tm")
    return lax.ppermute(block, "tm", [(i, i + 1) for i in range(size - 1)])


def to_earlier(block):
    size = lax.axis_size("tm")
    return lax.ppermute(block, "tm", [(i + 1, i) for i in range(size - 1)])


def by_tap(weight):
    return weight.reshape(4, 27, 8, CH).transpose(1, 0, 2, 3).reshape(864, CH)


def opening(x_ref, g_ref, w_ref, w2_ref, out_ref, both_ref):
    both_ref[:27] = w2_ref[...]
    both_ref[27:] = w_ref[...]
    total = None
    lane = iota((CH, 1024), 1)
    channel = ((lane >> 3) & 3) * 64 + (lane >> 7) * 8 + (lane & 7)
    hit = iota((CH, 1024), 0) == channel
    for a in range(4):
        place = (hit & (((lane >> 5) & 3) == a)).astype(F32).astype(BF16)
        rows = [w_ref[tap].astype(F32) for tap in range(a, 27, 4)]
        rows += [jnp.zeros((8, CH), F32)] * (8 - len(rows))
        term = mm(jnp.concatenate(rows, axis=0).astype(BF16), place, NN)
        total = term if total is None else total + term
    for owner in range(8):
        piece = total[:, owner * 128 : owner * 128 + 128].astype(BF16)
        out_ref[owner, :SHARD, :] = x_ref[...]
        out_ref[owner, SHARD : 2 * SHARD, :] = g_ref[...]
        out_ref[owner, 2 * SHARD :, :128] = piece[:32]
        out_ref[owner, 2 * SHARD :, 128:] = piece[32:]


def first_pieces(x_ref, out_ref):
    out_ref[...] = x_ref[:, 2 * SHARD :, :].reshape(CH, CH)


def first_stats(x_ref, row_ref):
    frames = [frame_of(x_ref, frame, 0).astype(F32) for frame in range(2)]
    same = ((iota((CH, CH), 0) >> 3) == (iota((CH, CH), 1) >> 3)).astype(F32)
    group = iota((CH, 128), 0) >> 3
    lane = iota((CH, 128), 1)
    sums = sum(jnp.sum(x, axis=0, keepdims=True) for x in frames)
    mean = exact(jnp.broadcast_to(sums, (8, CH)), same, NN)[:1] * (1.0 / (POS * 8))
    squares = sum(jnp.sum((x - mean) * (x - mean), axis=0, keepdims=True) for x in frames)
    means = exact(
        jnp.broadcast_to(mean, (8, CH)), ((group == lane) & ((iota((CH, 128), 0) & 7) == 0)).astype(F32), NN
    )
    spreads = exact(jnp.broadcast_to(squares, (8, CH)), (group + 32 == lane).astype(F32), NN)
    row_ref[...] = jnp.broadcast_to((means + spreads)[None, :1], row_ref.shape)


def turn_weight(w_ref, out_ref):
    eye = (iota((128, 128), 0) == iota((128, 128), 1)).astype(F32).astype(BF16)
    for part in range(7):
        out_ref[part * 128 : part * 128 + 128, :] = mm(eye, w_ref[part], NT).astype(BF16)


def order_weight(w_ref, out_ref):
    out_ref[...] = mm(w_ref[...], order_matrix(), NT).astype(BF16)


def shifted(value, by, keep):
    return jnp.where(keep, pltpu.roll(value, (-by) % IMG, 1), 0.0)


def fold(taps, sign, cols_ref):
    lane = iota((OWN, IMG), 1)
    col = jnp.broadcast_to(cols_ref[...], (OWN, IMG))
    keep_col = {1: col != COLS - 1, -1: col != 0}
    keep_row = {1: lane < IMG - COLS, -1: lane >= COLS}
    total = None
    for j in range(3):
        line = None
        for k in range(3):
            value = taps[(3 * j + k) * OWN : (3 * j + k + 1) * OWN, :]
            step = sign * (k - 1)
            if step:
                value = shifted(value, step, keep_col[step])
            line = value if line is None else line + value
        step = sign * (j - 1)
        if step:
            line = shifted(line, step * COLS, keep_row[step])
        total = line if total is None else total + line
    return total


def convolve(frames, weight, dims, forward, cols_ref, own_ref, other_ref):
    if forward:
        plan = [(2, [(0, 0), (1, 1)], other_ref, 0), (3, [(1, 0)], other_ref, 1),
                (0, [(0, 2)], own_ref, 0), (1, [(0, 1), (1, 2)], own_ref, 1)]
    else:
        plan = [(-2, [(0, 0)], other_ref, 0), (-1, [(0, 1), (1, 0)], other_ref, 1),
                (0, [(0, 2), (1, 1)], own_ref, 0), (1, [(1, 2)], own_ref, 1)]
    for _, terms, ref, slot in plan:
        taps = None
        for frame, time_tap in terms:
            term = mm(weight[time_tap * 288 : time_tap * 288 + 288, :], frames[frame], dims)
            taps = term if taps is None else taps + term
        value = fold(taps, 1 if forward else -1, cols_ref)
        ref[:OWN, slot * IMG : slot * IMG + IMG] = value.astype(ref.dtype)


def frame_of(ref, frame, base):
    start = base + frame * PART
    return ref[:, start : start + PART, :].reshape(IMG, CH)


def first_conv(h_ref, stats_ref, x_ref, w_ref, vec_ref, cols_ref, own_ref, pack_ref, column_ref):
    stats = stats_ref[...]
    lane = iota((16, 128), 1)
    mean = jnp.sum(stats, axis=0, keepdims=True) * (1.0 / 16)
    off = stats - mean
    spread_sum = jnp.sum(jnp.where(lane < 32, off * off * (POS * 8.0), stats), axis=0, keepdims=True)
    row = iota((8, 128), 0)
    lane8 = iota((8, 128), 1)
    both = jnp.where(row == 0, jnp.where(lane8 < 32, mean, 0.0), jnp.where(lane8 < 64, spread_sum, 0.0))
    expand = ((iota((128, CH), 0) & 31) == (iota((128, CH), 1) >> 3)).astype(F32)
    wide = exact(both, expand, NN)
    mean_c = wide[0:1]
    inv_c = lax.rsqrt(wide[1:2] * (1.0 / COUNT) + EPS)
    gain, shift = vec_ref[0:1], vec_ref[1:2]
    own = own_matrix(h_ref[0])
    row8 = iota((8, CH), 0)
    vectors = jnp.where(row8 == 4, mean_c, jnp.where(row8 == 5, inv_c, vec_ref[...]))
    columns = exact(own, vectors, NT)
    column_ref[...] = columns
    own16 = own.astype(BF16)
    acts = []
    for frame in range(2):
        raw = frame_of(x_ref, frame, 0)
        pack_ref[OWN:, frame * IMG : frame * IMG + IMG] = mm(own16, raw, NT).astype(BF16)
        pre = (raw.astype(F32) - mean_c) * inv_c * gain + shift
        acts.append((pre * jax.nn.sigmoid(pre)).astype(BF16))
    convolve(acts, w_ref, NT, True, cols_ref, own_ref, pack_ref)


def lanes_of(values):
    lane = iota((1, 128), 1)
    row = jnp.zeros((1, 128), F32)
    for n, value in enumerate(values):
        row = jnp.where(lane == n, value, row)
    return row


def lane_of(row, n):
    return jnp.sum(jnp.where(iota((1, 128), 1) == n, row, 0.0), axis=1, keepdims=True)


def total_of(value):
    return jnp.sum(jnp.sum(value, axis=1, keepdims=True), axis=0, keepdims=True)


def hidden_stats(own_ref, got_ref, hidden_ref, row_ref):
    hidden = (own_ref[...] + got_ref[:OWN, :].astype(F32)).astype(BF16)
    hidden_ref[...] = hidden
    means, spreads = [], []
    for g in range(4):
        value = hidden.astype(F32)[8 * g : 8 * g + 8]
        mean = total_of(value) * (1.0 / (8 * POS))
        off = value - mean
        means.append(mean)
        spreads.append(total_of(off * off))
    row_ref[...] = jnp.broadcast_to(lanes_of(means + spreads)[None], row_ref.shape)


def silu_slope(value):
    sigma = jax.nn.sigmoid(value)
    return sigma * (1.0 + value * (1.0 - sigma))


def second_conv(h_ref, g_ref, w_ref, cols_ref, own_ref, other_ref, grad_ref):
    own16 = own_matrix(h_ref[0]).astype(BF16)
    frames = [frame_of(g_ref, frame, SHARD) for frame in range(2)]
    convolve(frames, w_ref, NT, False, cols_ref, own_ref, other_ref)
    for frame in range(2):
        grad_ref[:, frame * IMG : frame * IMG + IMG] = mm(own16, frames[frame], NT)


def second_slope(stats_ref, hidden_ref, own_ref, got_ref, column_ref, slope_ref, normed_ref, inv_ref, row_ref):
    stats = stats_ref[...]
    mean_row = jnp.sum(stats, axis=0, keepdims=True) * (1.0 / 16)
    off = stats - mean_row
    between = jnp.sum(off * off, axis=0, keepdims=True) * (8.0 * POS)
    within = jnp.sum(stats, axis=0, keepdims=True)
    hidden = hidden_ref[...].astype(F32)
    grad = own_ref[...] + got_ref[...].astype(F32)
    firsts, seconds, invs = [], [], []
    for g in range(4):
        rows = slice(8 * g, 8 * g + 8)
        mean = lane_of(mean_row, g)
        inv = lax.rsqrt((lane_of(between, g) + lane_of(within, 4 + g)) * (1.0 / COUNT) + EPS)
        gain, shift = column_ref[rows, 2:3], column_ref[rows, 3:4]
        normed = (hidden[rows] - mean) * inv
        slope = grad[rows] * silu_slope(normed * gain + shift) * gain
        slope_ref[rows, :] = slope
        normed_ref[rows, :] = normed
        firsts.append(total_of(slope))
        seconds.append(total_of(slope * normed))
        invs.append(inv)
    inv_ref[...] = lanes_of(invs)
    row_ref[...] = jnp.broadcast_to(lanes_of(firsts + seconds)[None], row_ref.shape)


def hidden_grad(sums_ref, slope_ref, normed_ref, inv_ref, out_ref):
    means = jnp.sum(sums_ref[...], axis=0, keepdims=True) * (1.0 / COUNT)
    values = []
    for g in range(4):
        rows = slice(8 * g, 8 * g + 8)
        inv = lane_of(inv_ref[...], g)
        inner = slope_ref[rows, :] - lane_of(means, g) - normed_ref[rows, :] * lane_of(means, 4 + g)
        values.append(inv * inner)
    out_ref[...] = jnp.concatenate(values, axis=0).astype(BF16)


def third_conv(place_ref, g_ref, w_ref, cols_ref, pack_ref, before_ref, column_ref, own_ref, other_ref, factor_ref, normed_ref, row_ref):
    frames = [
        g_ref[:, :, frame * IMG : frame * IMG + IMG].reshape(CH, IMG) for frame in range(2)
    ]
    convolve(frames, w_ref, NN, False, cols_ref, own_ref, other_ref)
    gain, shift = column_ref[:, 0:1], column_ref[:, 1:2]
    mean, inv = column_ref[:, 4:5], column_ref[:, 5:6]
    normed = (pack_ref[OWN:, :].astype(F32) - mean) * inv
    factor = silu_slope(normed * gain + shift) * gain
    normed_before = (before_ref[OWN:, :].astype(F32) - mean) * inv
    factor_before = silu_slope(normed_before * gain + shift) * gain
    factor_ref[...] = factor
    normed_ref[...] = normed
    slope = own_ref[...] * factor
    slope_before = jnp.where(place_ref[1] > 0, other_ref[...].astype(F32) * factor_before, 0.0)
    first = slope + slope_before
    second = slope * normed + slope_before * normed_before
    sums = lanes_of([total_of(value[8 * g : 8 * g + 8]) for value in (first, second) for g in range(4)])
    row_ref[...] = jnp.broadcast_to(sums[None], row_ref.shape)


def input_grad(sums_ref, own_ref, got_ref, factor_ref, normed_ref, column_ref, grad_ref, out_ref):
    means = jnp.sum(sums_ref[...], axis=0, keepdims=True) * (1.0 / COUNT)
    border = got_ref[...].astype(F32)
    values = []
    for g in range(4):
        rows = slice(8 * g, 8 * g + 8)
        slope = (own_ref[rows, :] + border[rows]) * factor_ref[rows, :]
        inner = slope - lane_of(means, g) - normed_ref[rows, :] * lane_of(means, 4 + g)
        values.append(grad_ref[rows, :] + column_ref[rows, 5:6] * inner)
    value = jnp.concatenate(values, axis=0)
    for frame in range(2):
        image = value[:, frame * IMG : frame * IMG + IMG]
        for owner in range(8):
            moved = pltpu.roll(image, (-owner * PART) % IMG, 1) if owner else image
            out_ref[owner, :, frame * 128 : frame * 128 + 128] = moved[:, :128].astype(BF16)


def gather_rows(got_ref, out_ref):
    order = order_matrix()
    for frame in range(2):
        value = got_ref[:, :, frame * 128 : frame * 128 + 128].reshape(CH, 128)
        out_ref[frame * PART : frame * PART + PART, :] = mm(value, order, TN)[:PART].astype(BF16)


def on_device(inputs, grad_out, conv1_weight, conv2_weight, gain1, shift1, gain2, shift2):
    x = inputs.reshape(SHARD, CH)
    upstream = grad_out.reshape(SHARD, CH)
    place = jnp.stack([lax.axis_index("height"), lax.axis_index("tm")]).astype(jnp.int32)
    cols = jnp.asarray(np.arange(IMG)[None, :] % COLS, jnp.int32)
    zero = jnp.zeros_like(gain1)
    vectors = jnp.stack([gain1, shift1, gain2, shift2, zero, zero, zero, zero])
    half = shape(OWN, POS)
    rows16 = shape(16, 1, 128)
    half16 = shape(OWN, POS, dtype=BF16)

    parcel, both = call(
        opening,
        [shape(8, 2 * SHARD + 32, CH, dtype=BF16), shape(54, 8, CH, dtype=BF16)],
        x, upstream, conv1_weight.reshape(27, 8, CH), conv2_weight.reshape(27, 8, CH), vmem_mib=60,
    )
    all_rows = lax.all_to_all(parcel, "height", 0, 0, tiled=True)
    both = lax.all_gather(both.reshape(432, CH), "dp")
    w1_back = call(order_weight, shape(864, CH, dtype=BF16), by_tap(both[:, 216:]))
    w2_back = by_tap(both[:, :216])
    stats1 = call(first_stats, rows16, all_rows)
    all_rows, stats1 = lax.optimization_barrier((all_rows, stats1))
    pieces = call(first_pieces, shape(CH, CH, dtype=BF16), all_rows, flops=3 * 10**10)
    stats1 = exchanged(stats1, "tm")
    pieces = lax.all_gather(pieces, "dp")
    pieces = pieces.reshape(4, 8, 4, 8, 2, 128).transpose(4, 2, 0, 1, 3, 5).reshape(8, CH, 128)
    w1_forward = call(turn_weight, shape(896, CH, dtype=BF16), pieces)
    own, pack, columns = call(
        first_conv, [half, shape(2 * OWN, POS, dtype=BF16), shape(OWN, 8)], place, stats1, all_rows, w1_forward, vectors, cols, smem=1
    )
    before = to_later(pack)
    w2_back, _ = lax.optimization_barrier((w2_back, columns))
    own2, other2, grad_t = call(second_conv, [half, half16, half], place, all_rows, w2_back, cols, smem=1)
    got2 = to_earlier(other2)
    hidden, stats2 = call(hidden_stats, [half16, rows16], own, before)
    stats2 = exchanged(stats2, "tm")
    slope2, normed2, inv2, sums2 = call(
        second_slope, [half, half, shape(1, 128), rows16], stats2, hidden, own2, got2, columns
    )
    sums2 = exchanged(sums2, "tm")
    grad_hidden = call(hidden_grad, half16, sums2, slope2, normed2, inv2)
    grad_hidden = lax.all_gather(grad_hidden, "height")
    own, other, factor1, normed1, sums1 = call(
        third_conv, [half, half16, half, half, rows16], place, grad_hidden, w1_back, cols, pack, before, columns, smem=1
    )
    got = to_earlier(other)
    sums1 = exchanged(sums1, "tm")
    result = call(
        input_grad, shape(8, OWN, 256, dtype=BF16), sums1, own, got, factor1, normed1, columns, grad_t
    )
    result = lax.all_to_all(result, "height", 0, 0, tiled=True)
    return call(gather_rows, shape(SHARD, CH, dtype=BF16), result).reshape(inputs.shape)


def solution(mesh):
    return jax.shard_map(
        on_device,
        mesh=mesh,
        in_specs=(
            P("dp", "tm", "height", None, None),
            P("dp", "tm", "height", None, None),
            P(None, None, ("dp", "height"), None),
            P(None, None, ("dp", "height"), None),
            P(),
            P(),
            P(),
            P(),
        ),
        out_specs=P("dp", "tm", "height", None, None),
        check_vma=False,
    )
```

```python
import jax
import jax.numpy as jnp
import numpy as np
from jax import lax
from jax.experimental import pallas as pl
from jax.experimental.pallas import tpu as pltpu
from jax.sharding import PartitionSpec as P

EPS = 1e-06
F32 = jnp.float32
BF16 = jnp.bfloat16
CH = 256
OWN = 32
COLS = 40
IMG = 640
POS = 2 * IMG
SHARD = 160
PART = 80
COUNT = 32 * IMG * 8


def iota(shape, dim):
    return lax.broadcasted_iota(jnp.int32, shape, dim)


def exact(a, b, dims):
    return lax.dot_general(
        a, b, (dims, ((), ())), precision=lax.Precision.HIGHEST, preferred_element_type=F32
    )


def mm(a, b, dims):
    return lax.dot_general(a, b, (dims, ((), ())), preferred_element_type=F32)


NT = ((1,), (1,))
NN = ((1,), (0,))
TN = ((0,), (0,))


def channel_of(index):
    return ((index >> 3) & 3) * 64 + (index >> 5) * 8 + (index & 7)


def order_matrix():
    return (iota((CH, CH), 1) == channel_of(iota((CH, CH), 0))).astype(F32).astype(BF16)


def own_matrix(h):
    place = iota((OWN, CH), 0)
    return (iota((OWN, CH), 1) == (place >> 3) * 64 + h * 8 + (place & 7)).astype(F32)


def call(kernel, outs, *args, smem=0, vmem_mib=32, flops=10**7):
    many = isinstance(outs, (list, tuple))
    specs = [pl.BlockSpec(memory_space=pltpu.SMEM)] * smem
    specs += [pl.BlockSpec(memory_space=pltpu.VMEM)] * (len(args) - smem)
    vmem = pl.BlockSpec(memory_space=pltpu.VMEM)
    return pl.pallas_call(
        kernel,
        out_shape=outs,
        in_specs=specs,
        out_specs=[vmem] * len(outs) if many else vmem,
        compiler_params=pltpu.CompilerParams(vmem_limit_bytes=vmem_mib * 2**20),
        cost_estimate=pl.CostEstimate(flops=flops, bytes_accessed=10**6, transcendentals=0),
    )(*args)


def shape(*dims, dtype=F32):
    return jax.ShapeDtypeStruct(dims, dtype)


def exchanged(rows, first=0):
    size = rows.shape[0]
    order = [(first + i) % size for i in range(size)]
    got = lax.all_to_all(rows, "tm", 0, 0, axis_index_groups=[order] if first else None, tiled=True)
    return got.reshape(size, 128)


def to_later(block):
    size = lax.axis_size("tm")
    return lax.ppermute(block, "tm", [(i, i + 1) for i in range(size - 1)])


def to_earlier(block):
    size = lax.axis_size("tm")
    return lax.ppermute(block, "tm", [(i + 1, i) for i in range(size - 1)])


def by_tap(weight):
    return weight.reshape(4, 27, 8, CH).transpose(1, 0, 2, 3).reshape(864, CH)


def opening(x_ref, g_ref, w_ref, w2_ref, out_ref, both_ref):
    both_ref[:27] = w2_ref[...]
    both_ref[27:] = w_ref[...]
    total = None
    lane = iota((CH, 1024), 1)
    channel = ((lane >> 3) & 3) * 64 + (lane >> 7) * 8 + (lane & 7)
    hit = iota((CH, 1024), 0) == channel
    for a in range(4):
        place = (hit & (((lane >> 5) & 3) == a)).astype(F32).astype(BF16)
        rows = [w_ref[tap].astype(F32) for tap in range(a, 27, 4)]
        rows += [jnp.zeros((8, CH), F32)] * (8 - len(rows))
        term = mm(jnp.concatenate(rows, axis=0).astype(BF16), place, NN)
        total = term if total is None else total + term
    for owner in range(8):
        piece = total[:, owner * 128 : owner * 128 + 128].astype(BF16)
        out_ref[owner, :SHARD, :] = x_ref[...]
        out_ref[owner, SHARD : 2 * SHARD, :] = g_ref[...]
        out_ref[owner, 2 * SHARD :, :128] = piece[:32]
        out_ref[owner, 2 * SHARD :, 128:] = piece[32:]


def first_pieces(x_ref, out_ref):
    out_ref[...] = x_ref[:, 2 * SHARD :, :].reshape(CH, CH)


def group_sums(row):
    lane = iota(row.shape, 1)
    for step in (1, 2, 4):
        row = row + jnp.where((lane & step) == 0, pltpu.roll(row, CH - step, 1), pltpu.roll(row, step, 1))
    return row


def first_stats(x_ref, row_ref):
    frames = [frame_of(x_ref, frame, 0).astype(F32) for frame in range(2)]
    sums = sum(jnp.sum(x, axis=0, keepdims=True) for x in frames)
    mean = group_sums(sums) * (1.0 / (POS * 8))
    squares = group_sums(sum(jnp.sum((x - mean) * (x - mean), axis=0, keepdims=True) for x in frames))
    row = iota((8, CH), 0)
    both = jnp.where(row == 0, mean, jnp.where(row == 1, squares, 0.0))
    pick = (iota((CH, 128), 0) == 8 * iota((CH, 128), 1)).astype(F32)
    both = exact(both, pick, NN)
    both = both[:1] + pltpu.roll(both, 32, 1)[1:2]
    row_ref[...] = jnp.broadcast_to(both[None], row_ref.shape)


def turn_weight(w_ref, out_ref):
    eye = (iota((128, 128), 0) == iota((128, 128), 1)).astype(F32).astype(BF16)
    for part in range(7):
        out_ref[part * 128 : part * 128 + 128, :] = mm(eye, w_ref[part], NT).astype(BF16)


def order_weight(w_ref, out_ref):
    out_ref[...] = mm(w_ref[...], order_matrix(), NT).astype(BF16)


def shifted(value, by, keep):
    return jnp.where(keep, pltpu.roll(value, (-by) % IMG, 1), 0.0)


def fold(taps, sign, cols_ref):
    lane = iota((OWN, IMG), 1)
    col = jnp.broadcast_to(cols_ref[...], (OWN, IMG))
    keep_col = {1: col != COLS - 1, -1: col != 0}
    keep_row = {1: lane < IMG - COLS, -1: lane >= COLS}
    total = None
    for j in range(3):
        line = None
        for k in range(3):
            value = taps[(3 * j + k) * OWN : (3 * j + k + 1) * OWN, :]
            step = sign * (k - 1)
            if step:
                value = shifted(value, step, keep_col[step])
            line = value if line is None else line + value
        step = sign * (j - 1)
        if step:
            line = shifted(line, step * COLS, keep_row[step])
        total = line if total is None else total + line
    return total


def convolve(frames, weight, dims, forward, cols_ref, own_ref, other_ref):
    if forward:
        plan = [(2, [(0, 0), (1, 1)], other_ref, 0), (3, [(1, 0)], other_ref, 1),
                (0, [(0, 2)], own_ref, 0), (1, [(0, 1), (1, 2)], own_ref, 1)]
    else:
        plan = [(-2, [(0, 0)], other_ref, 0), (-1, [(0, 1), (1, 0)], other_ref, 1),
                (0, [(0, 2), (1, 1)], own_ref, 0), (1, [(1, 2)], own_ref, 1)]
    for _, terms, ref, slot in plan:
        taps = None
        for frame, time_tap in terms:
            term = mm(weight[time_tap * 288 : time_tap * 288 + 288, :], frames[frame], dims)
            taps = term if taps is None else taps + term
        value = fold(taps, 1 if forward else -1, cols_ref)
        ref[:OWN, slot * IMG : slot * IMG + IMG] = value.astype(ref.dtype)


def frame_of(ref, frame, base):
    start = base + frame * PART
    return ref[:, start : start + PART, :].reshape(IMG, CH)


def first_conv(h_ref, stats_ref, x_ref, w_ref, vec_ref, cols_ref, own_ref, pack_ref, column_ref):
    stats = stats_ref[...]
    lane = iota((16, 128), 1)
    mean = jnp.sum(stats, axis=0, keepdims=True) * (1.0 / 16)
    off = stats - mean
    spread_sum = jnp.sum(jnp.where(lane < 32, off * off * (POS * 8.0), stats), axis=0, keepdims=True)
    row = iota((8, 128), 0)
    lane8 = iota((8, 128), 1)
    both = jnp.where(row == 0, jnp.where(lane8 < 32, mean, 0.0), jnp.where(lane8 < 64, spread_sum, 0.0))
    expand = ((iota((128, CH), 0) & 31) == (iota((128, CH), 1) >> 3)).astype(F32)
    wide = exact(both, expand, NN)
    mean_c = wide[0:1]
    inv_c = lax.rsqrt(wide[1:2] * (1.0 / COUNT) + EPS)
    gain, shift = vec_ref[0:1], vec_ref[1:2]
    own = own_matrix(h_ref[0])
    row8 = iota((8, CH), 0)
    vectors = jnp.where(row8 == 4, mean_c, jnp.where(row8 == 5, inv_c, vec_ref[...]))
    columns = exact(own, vectors, NT)
    column_ref[...] = columns
    own16 = own.astype(BF16)
    acts = []
    for frame in range(2):
        raw = frame_of(x_ref, frame, 0)
        pack_ref[OWN:, frame * IMG : frame * IMG + IMG] = mm(own16, raw, NT).astype(BF16)
        pre = (raw.astype(F32) - mean_c) * inv_c * gain + shift
        acts.append((pre * jax.nn.sigmoid(pre)).astype(BF16))
    convolve(acts, w_ref, NT, True, cols_ref, own_ref, pack_ref)


def lanes_of(values):
    lane = iota((1, 128), 1)
    row = jnp.zeros((1, 128), F32)
    for n, value in enumerate(values):
        row = jnp.where(lane == n, value, row)
    return row


def lane_of(row, n):
    return jnp.sum(jnp.where(iota((1, 128), 1) == n, row, 0.0), axis=1, keepdims=True)


def total_of(value):
    return jnp.sum(jnp.sum(value, axis=1, keepdims=True), axis=0, keepdims=True)


def hidden_stats(own_ref, got_ref, hidden_ref, row_ref):
    hidden = (own_ref[...] + got_ref[:OWN, :].astype(F32)).astype(BF16)
    hidden_ref[...] = hidden
    means, spreads = [], []
    for g in range(4):
        value = hidden.astype(F32)[8 * g : 8 * g + 8]
        mean = total_of(value) * (1.0 / (8 * POS))
        off = value - mean
        means.append(mean)
        spreads.append(total_of(off * off))
    row_ref[...] = jnp.broadcast_to(lanes_of(means + spreads)[None], row_ref.shape)


def silu_slope(value):
    sigma = jax.nn.sigmoid(value)
    return sigma * (1.0 + value * (1.0 - sigma))


def second_conv(h_ref, g_ref, w_ref, cols_ref, own_ref, other_ref, grad_ref):
    own16 = own_matrix(h_ref[0]).astype(BF16)
    frames = [frame_of(g_ref, frame, SHARD) for frame in range(2)]
    convolve(frames, w_ref, NT, False, cols_ref, own_ref, other_ref)
    for frame in range(2):
        grad_ref[:, frame * IMG : frame * IMG + IMG] = mm(own16, frames[frame], NT)


def second_slope(stats_ref, hidden_ref, own_ref, got_ref, column_ref, slope_ref, normed_ref, inv_ref, row_ref):
    stats = stats_ref[...]
    mean_row = jnp.sum(stats, axis=0, keepdims=True) * (1.0 / 16)
    off = stats - mean_row
    between = jnp.sum(off * off, axis=0, keepdims=True) * (8.0 * POS)
    within = jnp.sum(stats, axis=0, keepdims=True)
    hidden = hidden_ref[...].astype(F32)
    grad = own_ref[...] + got_ref[...].astype(F32)
    firsts, seconds, invs = [], [], []
    for g in range(4):
        rows = slice(8 * g, 8 * g + 8)
        mean = lane_of(mean_row, g)
        inv = lax.rsqrt((lane_of(between, g) + lane_of(within, 4 + g)) * (1.0 / COUNT) + EPS)
        gain, shift = column_ref[rows, 2:3], column_ref[rows, 3:4]
        normed = (hidden[rows] - mean) * inv
        slope = grad[rows] * silu_slope(normed * gain + shift) * gain
        slope_ref[rows, :] = slope
        normed_ref[rows, :] = normed
        firsts.append(total_of(slope))
        seconds.append(total_of(slope * normed))
        invs.append(inv)
    inv_ref[...] = lanes_of(invs)
    row_ref[...] = jnp.broadcast_to(lanes_of(firsts + seconds)[None], row_ref.shape)


def hidden_grad(sums_ref, slope_ref, normed_ref, inv_ref, out_ref):
    means = jnp.sum(sums_ref[...], axis=0, keepdims=True) * (1.0 / COUNT)
    values = []
    for g in range(4):
        rows = slice(8 * g, 8 * g + 8)
        inv = lane_of(inv_ref[...], g)
        inner = slope_ref[rows, :] - lane_of(means, g) - normed_ref[rows, :] * lane_of(means, 4 + g)
        values.append(inv * inner)
    out_ref[...] = jnp.concatenate(values, axis=0).astype(BF16)


def third_conv(place_ref, g_ref, w_ref, cols_ref, pack_ref, before_ref, column_ref, own_ref, other_ref, factor_ref, normed_ref, row_ref):
    frames = [
        g_ref[:, :, frame * IMG : frame * IMG + IMG].reshape(CH, IMG) for frame in range(2)
    ]
    convolve(frames, w_ref, NN, False, cols_ref, own_ref, other_ref)
    gain, shift = column_ref[:, 0:1], column_ref[:, 1:2]
    mean, inv = column_ref[:, 4:5], column_ref[:, 5:6]
    normed = (pack_ref[OWN:, :].astype(F32) - mean) * inv
    factor = silu_slope(normed * gain + shift) * gain
    normed_before = (before_ref[OWN:, :].astype(F32) - mean) * inv
    factor_before = silu_slope(normed_before * gain + shift) * gain
    factor_ref[...] = factor
    normed_ref[...] = normed
    slope = own_ref[...] * factor
    slope_before = jnp.where(place_ref[1] > 0, other_ref[...].astype(F32) * factor_before, 0.0)
    first = slope + slope_before
    second = slope * normed + slope_before * normed_before
    sums = lanes_of([total_of(value[8 * g : 8 * g + 8]) for value in (first, second) for g in range(4)])
    row_ref[...] = jnp.broadcast_to(sums[None], row_ref.shape)


def input_grad(sums_ref, own_ref, got_ref, factor_ref, normed_ref, column_ref, grad_ref, out_ref):
    means = jnp.sum(sums_ref[...], axis=0, keepdims=True) * (1.0 / COUNT)
    border = got_ref[...].astype(F32)
    values = []
    for g in range(4):
        rows = slice(8 * g, 8 * g + 8)
        slope = (own_ref[rows, :] + border[rows]) * factor_ref[rows, :]
        inner = slope - lane_of(means, g) - normed_ref[rows, :] * lane_of(means, 4 + g)
        values.append(grad_ref[rows, :] + column_ref[rows, 5:6] * inner)
    value = jnp.concatenate(values, axis=0)
    for frame in range(2):
        image = value[:, frame * IMG : frame * IMG + IMG]
        for owner in range(8):
            moved = pltpu.roll(image, (-owner * PART) % IMG, 1) if owner else image
            out_ref[owner, :, frame * 128 : frame * 128 + 128] = moved[:, :128].astype(BF16)


def gather_rows(got_ref, out_ref):
    order = order_matrix()
    for frame in range(2):
        value = got_ref[:, :, frame * 128 : frame * 128 + 128].reshape(CH, 128)
        out_ref[frame * PART : frame * PART + PART, :] = mm(value, order, TN)[:PART].astype(BF16)


def on_device(inputs, grad_out, conv1_weight, conv2_weight, gain1, shift1, gain2, shift2):
    x = inputs.reshape(SHARD, CH)
    upstream = grad_out.reshape(SHARD, CH)
    place = jnp.stack([lax.axis_index("height"), lax.axis_index("tm")]).astype(jnp.int32)
    cols = jnp.asarray(np.arange(IMG)[None, :] % COLS, jnp.int32)
    zero = jnp.zeros_like(gain1)
    vectors = jnp.stack([gain1, shift1, gain2, shift2, zero, zero, zero, zero])
    half = shape(OWN, POS)
    rows16 = shape(16, 1, 128)
    half16 = shape(OWN, POS, dtype=BF16)

    parcel, both = call(
        opening,
        [shape(8, 2 * SHARD + 32, CH, dtype=BF16), shape(54, 8, CH, dtype=BF16)],
        x, upstream, conv1_weight.reshape(27, 8, CH), conv2_weight.reshape(27, 8, CH), vmem_mib=60,
    )
    all_rows = lax.all_to_all(parcel, "height", 0, 0, tiled=True)
    both = lax.all_gather(both.reshape(432, CH), "dp")
    w1_back = call(order_weight, shape(864, CH, dtype=BF16), by_tap(both[:, 216:]))
    w2_back = by_tap(both[:, :216])
    stats1 = call(first_stats, rows16, all_rows)
    all_rows, stats1 = lax.optimization_barrier((all_rows, stats1))
    pieces = call(first_pieces, shape(CH, CH, dtype=BF16), all_rows, flops=3 * 10**10)
    stats1 = exchanged(stats1, 8)
    pieces = lax.all_gather(pieces, "dp")
    pieces = pieces.reshape(4, 8, 4, 8, 2, 128).transpose(4, 2, 0, 1, 3, 5).reshape(8, CH, 128)
    w1_forward = call(turn_weight, shape(896, CH, dtype=BF16), pieces)
    own, pack, columns = call(
        first_conv, [half, shape(2 * OWN, POS, dtype=BF16), shape(OWN, 8)], place, stats1, all_rows, w1_forward, vectors, cols, smem=1
    )
    before = to_later(pack)
    w2_back, _ = lax.optimization_barrier((w2_back, columns))
    own2, other2, grad_t = call(second_conv, [half, half16, half], place, all_rows, w2_back, cols, smem=1)
    got2 = to_earlier(other2)
    hidden, stats2 = call(hidden_stats, [half16, rows16], own, before)
    stats2 = exchanged(stats2, 8)
    slope2, normed2, inv2, sums2 = call(
        second_slope, [half, half, shape(1, 128), rows16], stats2, hidden, own2, got2, columns
    )
    sums2 = exchanged(sums2, 8)
    grad_hidden = call(hidden_grad, half16, sums2, slope2, normed2, inv2)
    grad_hidden = lax.all_gather(grad_hidden, "height")
    own, other, factor1, normed1, sums1 = call(
        third_conv, [half, half16, half, half, rows16], place, grad_hidden, w1_back, cols, pack, before, columns, smem=1
    )
    got = to_earlier(other)
    sums1 = exchanged(sums1, 8)
    result = call(
        input_grad, shape(8, OWN, 256, dtype=BF16), sums1, own, got, factor1, normed1, columns, grad_t
    )
    result = lax.all_to_all(result, "height", 0, 0, tiled=True)
    return call(gather_rows, shape(SHARD, CH, dtype=BF16), result).reshape(inputs.shape)


def solution(mesh):
    return jax.shard_map(
        on_device,
        mesh=mesh,
        in_specs=(
            P("dp", "tm", "height", None, None),
            P("dp", "tm", "height", None, None),
            P(None, None, ("dp", "height"), None),
            P(None, None, ("dp", "height"), None),
            P(),
            P(),
            P(),
            P(),
        ),
        out_specs=P("dp", "tm", "height", None, None),
        check_vma=False,
    )
```

```python
import jax
import jax.numpy as jnp
import numpy as np
from jax import lax
from jax.experimental import pallas as pl
from jax.experimental.pallas import tpu as pltpu
from jax.sharding import PartitionSpec as P

EPS = 1e-06
F32 = jnp.float32
BF16 = jnp.bfloat16
CH = 256
OWN = 32
COLS = 40
IMG = 640
POS = 2 * IMG
SHARD = 160
PART = 80
COUNT = 32 * IMG * 8


def iota(shape, dim):
    return lax.broadcasted_iota(jnp.int32, shape, dim)


def exact(a, b, dims):
    return lax.dot_general(
        a, b, (dims, ((), ())), precision=lax.Precision.HIGHEST, preferred_element_type=F32
    )


def mm(a, b, dims):
    return lax.dot_general(a, b, (dims, ((), ())), preferred_element_type=F32)


NT = ((1,), (1,))
NN = ((1,), (0,))
TN = ((0,), (0,))


def channel_of(index):
    return ((index >> 3) & 3) * 64 + (index >> 5) * 8 + (index & 7)


def order_matrix():
    return (iota((CH, CH), 1) == channel_of(iota((CH, CH), 0))).astype(F32).astype(BF16)


def own_matrix(h):
    place = iota((OWN, CH), 0)
    return (iota((OWN, CH), 1) == (place >> 3) * 64 + h * 8 + (place & 7)).astype(F32)


def call(kernel, outs, *args, smem=0, vmem_mib=32, flops=10**7):
    many = isinstance(outs, (list, tuple))
    specs = [pl.BlockSpec(memory_space=pltpu.SMEM)] * smem
    specs += [pl.BlockSpec(memory_space=pltpu.VMEM)] * (len(args) - smem)
    vmem = pl.BlockSpec(memory_space=pltpu.VMEM)
    return pl.pallas_call(
        kernel,
        out_shape=outs,
        in_specs=specs,
        out_specs=[vmem] * len(outs) if many else vmem,
        compiler_params=pltpu.CompilerParams(vmem_limit_bytes=vmem_mib * 2**20),
        cost_estimate=pl.CostEstimate(flops=flops, bytes_accessed=10**6, transcendentals=0),
    )(*args)


def shape(*dims, dtype=F32):
    return jax.ShapeDtypeStruct(dims, dtype)


def exchanged(rows, first=0):
    size = rows.shape[0]
    order = [(first + i) % size for i in range(size)]
    got = lax.all_to_all(rows, "tm", 0, 0, axis_index_groups=[order] if first else None, tiled=True)
    return got.reshape(size, 128)


def to_later(block):
    size = lax.axis_size("tm")
    return lax.ppermute(block, "tm", [(i, i + 1) for i in range(size - 1)])


def to_earlier(block):
    size = lax.axis_size("tm")
    return lax.ppermute(block, "tm", [(i + 1, i) for i in range(size - 1)])


def by_tap(weight):
    return weight.reshape(4, 27, 8, CH).transpose(1, 0, 2, 3).reshape(864, CH)


def opening(x_ref, g_ref, w_ref, w2_ref, out_ref, both_ref):
    both_ref[:27] = w2_ref[...]
    both_ref[27:] = w_ref[...]
    total = None
    lane = iota((CH, 1024), 1)
    channel = ((lane >> 3) & 3) * 64 + (lane >> 7) * 8 + (lane & 7)
    hit = iota((CH, 1024), 0) == channel
    for a in range(4):
        place = (hit & (((lane >> 5) & 3) == a)).astype(F32).astype(BF16)
        rows = [w_ref[tap].astype(F32) for tap in range(a, 27, 4)]
        rows += [jnp.zeros((8, CH), F32)] * (8 - len(rows))
        term = mm(jnp.concatenate(rows, axis=0).astype(BF16), place, NN)
        total = term if total is None else total + term
    for owner in range(8):
        piece = total[:, owner * 128 : owner * 128 + 128].astype(BF16)
        out_ref[owner, :SHARD, :] = x_ref[...]
        out_ref[owner, SHARD : 2 * SHARD, :] = g_ref[...]
        out_ref[owner, 2 * SHARD :, :128] = piece[:32]
        out_ref[owner, 2 * SHARD :, 128:] = piece[32:]


def first_pieces(x_ref, out_ref):
    out_ref[...] = x_ref[:, 2 * SHARD :, :].reshape(CH, CH)


def group_sums(row):
    lane = iota(row.shape, 1)
    for step in (1, 2, 4):
        row = row + jnp.where((lane & step) == 0, pltpu.roll(row, CH - step, 1), pltpu.roll(row, step, 1))
    return row


def first_stats(x_ref, row_ref):
    frames = [frame_of(x_ref, frame, 0).astype(F32) for frame in range(2)]
    sums = sum(jnp.sum(x, axis=0, keepdims=True) for x in frames)
    mean = group_sums(sums) * (1.0 / (POS * 8))
    squares = group_sums(sum(jnp.sum((x - mean) * (x - mean), axis=0, keepdims=True) for x in frames))
    row = iota((8, CH), 0)
    both = jnp.where(row == 0, mean, jnp.where(row == 1, squares, 0.0))
    pick = (iota((CH, 128), 0) == 8 * iota((CH, 128), 1)).astype(F32)
    both = exact(both, pick, NN)
    both = both[:1] + pltpu.roll(both, 32, 1)[1:2]
    row_ref[...] = jnp.broadcast_to(both[None], row_ref.shape)


def turn_weight(w_ref, out_ref):
    eye = (iota((128, 128), 0) == iota((128, 128), 1)).astype(F32).astype(BF16)
    for part in range(7):
        out_ref[part * 128 : part * 128 + 128, :] = mm(eye, w_ref[part], NT).astype(BF16)


def order_weight(w_ref, out_ref):
    out_ref[...] = mm(w_ref[...], order_matrix(), NT).astype(BF16)


def shifted(value, by, keep):
    return jnp.where(keep, pltpu.roll(value, (-by) % IMG, 1), 0.0)


def fold(taps, sign, cols_ref):
    lane = iota((OWN, IMG), 1)
    col = jnp.broadcast_to(cols_ref[...], (OWN, IMG))
    keep_col = {1: col != COLS - 1, -1: col != 0}
    keep_row = {1: lane < IMG - COLS, -1: lane >= COLS}
    total = None
    for j in range(3):
        line = None
        for k in range(3):
            value = taps[(3 * j + k) * OWN : (3 * j + k + 1) * OWN, :]
            step = sign * (k - 1)
            if step:
                value = shifted(value, step, keep_col[step])
            line = value if line is None else line + value
        step = sign * (j - 1)
        if step:
            line = shifted(line, step * COLS, keep_row[step])
        total = line if total is None else total + line
    return total


def convolve(frames, weight, dims, forward, cols_ref, own_ref, other_ref):
    if forward:
        plan = [(2, [(0, 0), (1, 1)], other_ref, 0), (3, [(1, 0)], other_ref, 1),
                (0, [(0, 2)], own_ref, 0), (1, [(0, 1), (1, 2)], own_ref, 1)]
    else:
        plan = [(-2, [(0, 0)], other_ref, 0), (-1, [(0, 1), (1, 0)], other_ref, 1),
                (0, [(0, 2), (1, 1)], own_ref, 0), (1, [(1, 2)], own_ref, 1)]
    for _, terms, ref, slot in plan:
        taps = None
        for frame, time_tap in terms:
            term = mm(weight[time_tap * 288 : time_tap * 288 + 288, :], frames[frame], dims)
            taps = term if taps is None else taps + term
        value = fold(taps, 1 if forward else -1, cols_ref)
        ref[:OWN, slot * IMG : slot * IMG + IMG] = value.astype(ref.dtype)


def frame_of(ref, frame, base):
    start = base + frame * PART
    return ref[:, start : start + PART, :].reshape(IMG, CH)


def first_conv(h_ref, stats_ref, x_ref, w_ref, vec_ref, cols_ref, own_ref, pack_ref, column_ref):
    stats = stats_ref[...]
    lane = iota((16, 128), 1)
    mean = jnp.sum(stats, axis=0, keepdims=True) * (1.0 / 16)
    off = stats - mean
    spread_sum = jnp.sum(jnp.where(lane < 32, off * off * (POS * 8.0), stats), axis=0, keepdims=True)
    row = iota((8, 128), 0)
    lane8 = iota((8, 128), 1)
    both = jnp.where(row == 0, jnp.where(lane8 < 32, mean, 0.0), jnp.where(lane8 < 64, spread_sum, 0.0))
    expand = ((iota((128, CH), 0) & 31) == (iota((128, CH), 1) >> 3)).astype(F32)
    wide = exact(both, expand, NN)
    mean_c = wide[0:1]
    inv_c = lax.rsqrt(wide[1:2] * (1.0 / COUNT) + EPS)
    gain, shift = vec_ref[0:1], vec_ref[1:2]
    own = own_matrix(h_ref[0])
    row8 = iota((8, CH), 0)
    vectors = jnp.where(row8 == 4, mean_c, jnp.where(row8 == 5, inv_c, vec_ref[...]))
    columns = exact(own, vectors, NT)
    column_ref[...] = columns
    own16 = own.astype(BF16)
    acts = []
    for frame in range(2):
        raw = frame_of(x_ref, frame, 0)
        pack_ref[OWN:, frame * IMG : frame * IMG + IMG] = mm(own16, raw, NT).astype(BF16)
        pre = (raw.astype(F32) - mean_c) * inv_c * gain + shift
        acts.append((pre * jax.nn.sigmoid(pre)).astype(BF16))
    convolve(acts, w_ref, NT, True, cols_ref, own_ref, pack_ref)


def lanes_of(values):
    lane = iota((1, 128), 1)
    row = jnp.zeros((1, 128), F32)
    for n, value in enumerate(values):
        row = jnp.where(lane == n, value, row)
    return row


def lane_of(row, n):
    return jnp.sum(jnp.where(iota((1, 128), 1) == n, row, 0.0), axis=1, keepdims=True)


def total_of(value):
    return jnp.sum(jnp.sum(value, axis=1, keepdims=True), axis=0, keepdims=True)


def hidden_stats(own_ref, got_ref, hidden_ref, row_ref):
    hidden = (own_ref[...] + got_ref[:OWN, :].astype(F32)).astype(BF16)
    hidden_ref[...] = hidden
    means, spreads = [], []
    for g in range(4):
        value = hidden.astype(F32)[8 * g : 8 * g + 8]
        mean = total_of(value) * (1.0 / (8 * POS))
        off = value - mean
        means.append(mean)
        spreads.append(total_of(off * off))
    row_ref[...] = jnp.broadcast_to(lanes_of(means + spreads)[None], row_ref.shape)


def silu_slope(value):
    sigma = jax.nn.sigmoid(value)
    return sigma * (1.0 + value * (1.0 - sigma))


def second_conv(h_ref, g_ref, w_ref, cols_ref, own_ref, other_ref, grad_ref):
    own16 = own_matrix(h_ref[0]).astype(BF16)
    frames = [frame_of(g_ref, frame, SHARD) for frame in range(2)]
    convolve(frames, w_ref, NT, False, cols_ref, own_ref, other_ref)
    for frame in range(2):
        grad_ref[:, frame * IMG : frame * IMG + IMG] = mm(own16, frames[frame], NT)


def second_slope(stats_ref, hidden_ref, own_ref, got_ref, column_ref, slope_ref, normed_ref, inv_ref, row_ref):
    stats = stats_ref[...]
    mean_row = jnp.sum(stats, axis=0, keepdims=True) * (1.0 / 16)
    off = stats - mean_row
    between = jnp.sum(off * off, axis=0, keepdims=True) * (8.0 * POS)
    within = jnp.sum(stats, axis=0, keepdims=True)
    hidden = hidden_ref[...].astype(F32)
    grad = own_ref[...] + got_ref[...].astype(F32)
    firsts, seconds, invs = [], [], []
    for g in range(4):
        rows = slice(8 * g, 8 * g + 8)
        mean = lane_of(mean_row, g)
        inv = lax.rsqrt((lane_of(between, g) + lane_of(within, 4 + g)) * (1.0 / COUNT) + EPS)
        gain, shift = column_ref[rows, 2:3], column_ref[rows, 3:4]
        normed = (hidden[rows] - mean) * inv
        slope = grad[rows] * silu_slope(normed * gain + shift) * gain
        slope_ref[rows, :] = slope
        normed_ref[rows, :] = normed
        firsts.append(total_of(slope))
        seconds.append(total_of(slope * normed))
        invs.append(inv)
    inv_ref[...] = lanes_of(invs)
    row_ref[...] = jnp.broadcast_to(lanes_of(firsts + seconds)[None], row_ref.shape)


def hidden_grad(sums_ref, slope_ref, normed_ref, inv_ref, out_ref):
    means = jnp.sum(sums_ref[...], axis=0, keepdims=True) * (1.0 / COUNT)
    values = []
    for g in range(4):
        rows = slice(8 * g, 8 * g + 8)
        inv = lane_of(inv_ref[...], g)
        inner = slope_ref[rows, :] - lane_of(means, g) - normed_ref[rows, :] * lane_of(means, 4 + g)
        values.append(inv * inner)
    out_ref[...] = jnp.concatenate(values, axis=0).astype(BF16)


def third_conv(place_ref, g_ref, w_ref, cols_ref, pack_ref, before_ref, column_ref, own_ref, other_ref, factor_ref, normed_ref, row_ref):
    frames = [
        g_ref[:, :, frame * IMG : frame * IMG + IMG].reshape(CH, IMG) for frame in range(2)
    ]
    convolve(frames, w_ref, NN, False, cols_ref, own_ref, other_ref)
    gain, shift = column_ref[:, 0:1], column_ref[:, 1:2]
    mean, inv = column_ref[:, 4:5], column_ref[:, 5:6]
    normed = (pack_ref[OWN:, :].astype(F32) - mean) * inv
    factor = silu_slope(normed * gain + shift) * gain
    normed_before = (before_ref[OWN:, :].astype(F32) - mean) * inv
    factor_before = silu_slope(normed_before * gain + shift) * gain
    factor_ref[...] = factor
    normed_ref[...] = normed
    slope = own_ref[...] * factor
    slope_before = jnp.where(place_ref[1] > 0, other_ref[...].astype(F32) * factor_before, 0.0)
    first = slope + slope_before
    second = slope * normed + slope_before * normed_before
    sums = lanes_of([total_of(value[8 * g : 8 * g + 8]) for value in (first, second) for g in range(4)])
    row_ref[...] = jnp.broadcast_to(sums[None], row_ref.shape)


def input_grad(sums_ref, own_ref, got_ref, factor_ref, normed_ref, column_ref, grad_ref, out_ref):
    means = jnp.sum(sums_ref[...], axis=0, keepdims=True) * (1.0 / COUNT)
    border = got_ref[...].astype(F32)
    values = []
    for g in range(4):
        rows = slice(8 * g, 8 * g + 8)
        slope = (own_ref[rows, :] + border[rows]) * factor_ref[rows, :]
        inner = slope - lane_of(means, g) - normed_ref[rows, :] * lane_of(means, 4 + g)
        values.append(grad_ref[rows, :] + column_ref[rows, 5:6] * inner)
    value = jnp.concatenate(values, axis=0)
    for frame in range(2):
        image = value[:, frame * IMG : frame * IMG + IMG]
        for owner in range(8):
            moved = pltpu.roll(image, (-owner * PART) % IMG, 1) if owner else image
            out_ref[owner, :, frame * 128 : frame * 128 + 128] = moved[:, :128].astype(BF16)


def gather_rows(got_ref, out_ref):
    order = order_matrix()
    for frame in range(2):
        value = got_ref[:, :, frame * 128 : frame * 128 + 128].reshape(CH, 128)
        out_ref[frame * PART : frame * PART + PART, :] = mm(value, order, TN)[:PART].astype(BF16)


def on_device(inputs, grad_out, conv1_weight, conv2_weight, gain1, shift1, gain2, shift2):
    x = inputs.reshape(SHARD, CH)
    upstream = grad_out.reshape(SHARD, CH)
    place = jnp.stack([lax.axis_index("height"), lax.axis_index("tm")]).astype(jnp.int32)
    cols = jnp.asarray(np.arange(IMG)[None, :] % COLS, jnp.int32)
    zero = jnp.zeros_like(gain1)
    vectors = jnp.stack([gain1, shift1, gain2, shift2, zero, zero, zero, zero])
    half = shape(OWN, POS)
    rows16 = shape(16, 1, 128)
    half16 = shape(OWN, POS, dtype=BF16)

    parcel, both = call(
        opening,
        [shape(8, 2 * SHARD + 32, CH, dtype=BF16), shape(54, 8, CH, dtype=BF16)],
        x, upstream, conv1_weight.reshape(27, 8, CH), conv2_weight.reshape(27, 8, CH), vmem_mib=60,
    )
    all_rows = lax.all_to_all(parcel, "height", 0, 0, tiled=True)
    both = lax.all_gather(both.reshape(432, CH), "dp")
    w1_back = call(order_weight, shape(864, CH, dtype=BF16), by_tap(both[:, 216:]))
    w2_back = by_tap(both[:, :216])
    stats1 = call(first_stats, rows16, all_rows)
    all_rows, stats1 = lax.optimization_barrier((all_rows, stats1))
    pieces = call(first_pieces, shape(CH, CH, dtype=BF16), all_rows, flops=3 * 10**10)
    stats1 = exchanged(stats1, 11)
    pieces = lax.all_gather(pieces, "dp")
    pieces = pieces.reshape(4, 8, 4, 8, 2, 128).transpose(4, 2, 0, 1, 3, 5).reshape(8, CH, 128)
    w1_forward = call(turn_weight, shape(896, CH, dtype=BF16), pieces)
    own, pack, columns = call(
        first_conv, [half, shape(2 * OWN, POS, dtype=BF16), shape(OWN, 8)], place, stats1, all_rows, w1_forward, vectors, cols, smem=1
    )
    before = to_later(pack)
    w2_back, _ = lax.optimization_barrier((w2_back, columns))
    own2, other2, grad_t = call(second_conv, [half, half16, half], place, all_rows, w2_back, cols, smem=1)
    got2 = to_earlier(other2)
    hidden, stats2 = call(hidden_stats, [half16, rows16], own, before)
    stats2 = exchanged(stats2, 4)
    slope2, normed2, inv2, sums2 = call(
        second_slope, [half, half, shape(1, 128), rows16], stats2, hidden, own2, got2, columns
    )
    sums2 = exchanged(sums2, 4)
    grad_hidden = call(hidden_grad, half16, sums2, slope2, normed2, inv2)
    grad_hidden = lax.all_gather(grad_hidden, "height")
    own, other, factor1, normed1, sums1 = call(
        third_conv, [half, half16, half, half, rows16], place, grad_hidden, w1_back, cols, pack, before, columns, smem=1
    )
    got = to_earlier(other)
    sums1 = exchanged(sums1, 8)
    result = call(
        input_grad, shape(8, OWN, 256, dtype=BF16), sums1, own, got, factor1, normed1, columns, grad_t
    )
    result = lax.all_to_all(result, "height", 0, 0, tiled=True)
    return call(gather_rows, shape(SHARD, CH, dtype=BF16), result).reshape(inputs.shape)


def solution(mesh):
    return jax.shard_map(
        on_device,
        mesh=mesh,
        in_specs=(
            P("dp", "tm", "height", None, None),
            P("dp", "tm", "height", None, None),
            P(None, None, ("dp", "height"), None),
            P(None, None, ("dp", "height"), None),
            P(),
            P(),
            P(),
            P(),
        ),
        out_specs=P("dp", "tm", "height", None, None),
        check_vma=False,
    )
```

```python
import jax
import jax.numpy as jnp
import numpy as np
from jax import lax
from jax.experimental import pallas as pl
from jax.experimental.pallas import tpu as pltpu
from jax.sharding import PartitionSpec as P

EPS = 1e-06
F32 = jnp.float32
BF16 = jnp.bfloat16
CH = 256
OWN = 32
COLS = 40
IMG = 640
POS = 2 * IMG
SHARD = 160
PART = 80
COUNT = 32 * IMG * 8


def iota(shape, dim):
    return lax.broadcasted_iota(jnp.int32, shape, dim)


def exact(a, b, dims):
    return lax.dot_general(
        a, b, (dims, ((), ())), precision=lax.Precision.HIGHEST, preferred_element_type=F32
    )


def mm(a, b, dims):
    return lax.dot_general(a, b, (dims, ((), ())), preferred_element_type=F32)


NT = ((1,), (1,))
NN = ((1,), (0,))
TN = ((0,), (0,))


def channel_of(index):
    return ((index >> 3) & 3) * 64 + (index >> 5) * 8 + (index & 7)


def order_matrix():
    return (iota((CH, CH), 1) == channel_of(iota((CH, CH), 0))).astype(F32).astype(BF16)


def own_matrix(h):
    place = iota((OWN, CH), 0)
    return (iota((OWN, CH), 1) == (place >> 3) * 64 + h * 8 + (place & 7)).astype(F32)


def call(kernel, outs, *args, smem=0, vmem_mib=32, flops=10**7):
    many = isinstance(outs, (list, tuple))
    specs = [pl.BlockSpec(memory_space=pltpu.SMEM)] * smem
    specs += [pl.BlockSpec(memory_space=pltpu.VMEM)] * (len(args) - smem)
    vmem = pl.BlockSpec(memory_space=pltpu.VMEM)
    return pl.pallas_call(
        kernel,
        out_shape=outs,
        in_specs=specs,
        out_specs=[vmem] * len(outs) if many else vmem,
        compiler_params=pltpu.CompilerParams(vmem_limit_bytes=vmem_mib * 2**20),
        cost_estimate=pl.CostEstimate(flops=flops, bytes_accessed=10**6, transcendentals=0),
    )(*args)


def shape(*dims, dtype=F32):
    return jax.ShapeDtypeStruct(dims, dtype)


def exchanged(rows, first=0):
    size = rows.shape[0]
    order = [(first + i) % size for i in range(size)]
    got = lax.all_to_all(rows, "tm", 0, 0, axis_index_groups=[order] if first else None, tiled=True)
    return got.reshape(size, 128)


def to_later(block):
    size = lax.axis_size("tm")
    return lax.ppermute(block, "tm", [(i, i + 1) for i in range(size - 1)])


def to_earlier(block):
    size = lax.axis_size("tm")
    return lax.ppermute(block, "tm", [(i + 1, i) for i in range(size - 1)])


def by_tap(weight):
    return weight.reshape(4, 27, 8, CH).transpose(1, 0, 2, 3).reshape(864, CH)


def opening(x_ref, g_ref, w_ref, w2_ref, out_ref, both_ref):
    both_ref[:27] = w2_ref[...]
    both_ref[27:] = w_ref[...]
    total = None
    lane = iota((CH, 1024), 1)
    channel = ((lane >> 3) & 3) * 64 + (lane >> 7) * 8 + (lane & 7)
    hit = iota((CH, 1024), 0) == channel
    for a in range(4):
        place = (hit & (((lane >> 5) & 3) == a)).astype(F32).astype(BF16)
        rows = [w_ref[tap].astype(F32) for tap in range(a, 27, 4)]
        rows += [jnp.zeros((8, CH), F32)] * (8 - len(rows))
        term = mm(jnp.concatenate(rows, axis=0).astype(BF16), place, NN)
        total = term if total is None else total + term
    for owner in range(8):
        piece = total[:, owner * 128 : owner * 128 + 128].astype(BF16)
        out_ref[owner, :SHARD, :] = x_ref[...]
        out_ref[owner, SHARD : 2 * SHARD, :] = g_ref[...]
        out_ref[owner, 2 * SHARD :, :128] = piece[:32]
        out_ref[owner, 2 * SHARD :, 128:] = piece[32:]


def first_pieces(x_ref, out_ref):
    out_ref[...] = x_ref[:, 2 * SHARD :, :].reshape(CH, CH)


def group_sums(row):
    lane = iota(row.shape, 1)
    for step in (1, 2, 4):
        row = row + jnp.where((lane & step) == 0, pltpu.roll(row, CH - step, 1), pltpu.roll(row, step, 1))
    return row


def first_stats(x_ref, row_ref):
    frames = [frame_of(x_ref, frame, 0).astype(F32) for frame in range(2)]
    sums = sum(jnp.sum(x, axis=0, keepdims=True) for x in frames)
    mean = group_sums(sums) * (1.0 / (POS * 8))
    squares = group_sums(sum(jnp.sum((x - mean) * (x - mean), axis=0, keepdims=True) for x in frames))
    row = iota((8, CH), 0)
    both = jnp.where(row == 0, mean, jnp.where(row == 1, squares, 0.0))
    pick = (iota((CH, 128), 0) == 8 * iota((CH, 128), 1)).astype(F32)
    both = exact(both, pick, NN)
    both = both[:1] + pltpu.roll(both, 32, 1)[1:2]
    row_ref[...] = jnp.broadcast_to(both[None], row_ref.shape)


def turn_weight(w_ref, out_ref):
    eye = (iota((128, 128), 0) == iota((128, 128), 1)).astype(F32).astype(BF16)
    for part in range(7):
        out_ref[part * 128 : part * 128 + 128, :] = mm(eye, w_ref[part], NT).astype(BF16)


def order_weight(w_ref, out_ref):
    out_ref[...] = mm(w_ref[...], order_matrix(), NT).astype(BF16)


def shifted(value, by, keep):
    return jnp.where(keep, pltpu.roll(value, (-by) % IMG, 1), 0.0)


def fold(taps, sign, cols_ref):
    lane = iota((OWN, IMG), 1)
    col = jnp.broadcast_to(cols_ref[...], (OWN, IMG))
    keep_col = {1: col != COLS - 1, -1: col != 0}
    keep_row = {1: lane < IMG - COLS, -1: lane >= COLS}
    total = None
    for j in range(3):
        line = None
        for k in range(3):
            value = taps[(3 * j + k) * OWN : (3 * j + k + 1) * OWN, :]
            step = sign * (k - 1)
            if step:
                value = shifted(value, step, keep_col[step])
            line = value if line is None else line + value
        step = sign * (j - 1)
        if step:
            line = shifted(line, step * COLS, keep_row[step])
        total = line if total is None else total + line
    return total


def convolve(frames, weight, dims, forward, cols_ref, own_ref, other_ref):
    if forward:
        plan = [(2, [(0, 0), (1, 1)], other_ref, 0), (3, [(1, 0)], other_ref, 1),
                (0, [(0, 2)], own_ref, 0), (1, [(0, 1), (1, 2)], own_ref, 1)]
    else:
        plan = [(-2, [(0, 0)], other_ref, 0), (-1, [(0, 1), (1, 0)], other_ref, 1),
                (0, [(0, 2), (1, 1)], own_ref, 0), (1, [(1, 2)], own_ref, 1)]
    for _, terms, ref, slot in plan:
        taps = None
        for frame, time_tap in terms:
            term = mm(weight[time_tap * 288 : time_tap * 288 + 288, :], frames[frame], dims)
            taps = term if taps is None else taps + term
        value = fold(taps, 1 if forward else -1, cols_ref)
        ref[:OWN, slot * IMG : slot * IMG + IMG] = value.astype(ref.dtype)


def frame_of(ref, frame, base):
    start = base + frame * PART
    return ref[:, start : start + PART, :].reshape(IMG, CH)


def first_conv(h_ref, stats_ref, x_ref, w_ref, vec_ref, cols_ref, own_ref, pack_ref, column_ref):
    stats = stats_ref[...]
    lane = iota((16, 128), 1)
    mean = jnp.sum(stats, axis=0, keepdims=True) * (1.0 / 16)
    off = stats - mean
    spread_sum = jnp.sum(jnp.where(lane < 32, off * off * (POS * 8.0), stats), axis=0, keepdims=True)
    row = iota((8, 128), 0)
    lane8 = iota((8, 128), 1)
    both = jnp.where(row == 0, jnp.where(lane8 < 32, mean, 0.0), jnp.where(lane8 < 64, spread_sum, 0.0))
    expand = ((iota((128, CH), 0) & 31) == (iota((128, CH), 1) >> 3)).astype(F32)
    wide = exact(both, expand, NN)
    mean_c = wide[0:1]
    inv_c = lax.rsqrt(wide[1:2] * (1.0 / COUNT) + EPS)
    gain, shift = vec_ref[0:1], vec_ref[1:2]
    own = own_matrix(h_ref[0])
    row8 = iota((8, CH), 0)
    vectors = jnp.where(row8 == 4, mean_c, jnp.where(row8 == 5, inv_c, vec_ref[...]))
    columns = exact(own, vectors, NT)
    column_ref[...] = columns
    own16 = own.astype(BF16)
    acts = []
    for frame in range(2):
        raw = frame_of(x_ref, frame, 0)
        pack_ref[OWN:, frame * IMG : frame * IMG + IMG] = mm(own16, raw, NT).astype(BF16)
        pre = (raw.astype(F32) - mean_c) * inv_c * gain + shift
        acts.append((pre * jax.nn.sigmoid(pre)).astype(BF16))
    convolve(acts, w_ref, NT, True, cols_ref, own_ref, pack_ref)


def lanes_of(values):
    lane = iota((1, 128), 1)
    row = jnp.zeros((1, 128), F32)
    for n, value in enumerate(values):
        row = jnp.where(lane == n, value, row)
    return row


def lane_of(row, n):
    return jnp.sum(jnp.where(iota((1, 128), 1) == n, row, 0.0), axis=1, keepdims=True)


def total_of(value):
    return jnp.sum(jnp.sum(value, axis=1, keepdims=True), axis=0, keepdims=True)


def hidden_stats(own_ref, got_ref, hidden_ref, row_ref):
    hidden = (own_ref[...] + got_ref[:OWN, :].astype(F32)).astype(BF16)
    hidden_ref[...] = hidden
    means, spreads = [], []
    for g in range(4):
        value = hidden.astype(F32)[8 * g : 8 * g + 8]
        mean = total_of(value) * (1.0 / (8 * POS))
        off = value - mean
        means.append(mean)
        spreads.append(total_of(off * off))
    row_ref[...] = jnp.broadcast_to(lanes_of(means + spreads)[None], row_ref.shape)


def silu_slope(value):
    sigma = jax.nn.sigmoid(value)
    return sigma * (1.0 + value * (1.0 - sigma))


def second_conv(h_ref, g_ref, w_ref, cols_ref, own_ref, other_ref, grad_ref):
    own16 = own_matrix(h_ref[0]).astype(BF16)
    frames = [frame_of(g_ref, frame, SHARD) for frame in range(2)]
    convolve(frames, w_ref, NT, False, cols_ref, own_ref, other_ref)
    for frame in range(2):
        grad_ref[:, frame * IMG : frame * IMG + IMG] = mm(own16, frames[frame], NT)


def widen(value_ref, out_ref):
    out_ref[...] = value_ref[...].astype(F32)


def second_slope(stats_ref, hidden_ref, own_ref, got_ref, column_ref, slope_ref, normed_ref, inv_ref, row_ref):
    stats = stats_ref[...]
    mean_row = jnp.sum(stats, axis=0, keepdims=True) * (1.0 / 16)
    off = stats - mean_row
    between = jnp.sum(off * off, axis=0, keepdims=True) * (8.0 * POS)
    within = jnp.sum(stats, axis=0, keepdims=True)
    hidden = hidden_ref[...]
    grad = own_ref[...] + got_ref[...].astype(F32)
    firsts, seconds, invs = [], [], []
    for g in range(4):
        rows = slice(8 * g, 8 * g + 8)
        mean = lane_of(mean_row, g)
        inv = lax.rsqrt((lane_of(between, g) + lane_of(within, 4 + g)) * (1.0 / COUNT) + EPS)
        gain, shift = column_ref[rows, 2:3], column_ref[rows, 3:4]
        normed = (hidden[rows] - mean) * inv
        slope = grad[rows] * silu_slope(normed * gain + shift) * gain
        slope_ref[rows, :] = slope
        normed_ref[rows, :] = normed
        firsts.append(total_of(slope))
        seconds.append(total_of(slope * normed))
        invs.append(inv)
    inv_ref[...] = lanes_of(invs)
    row_ref[...] = jnp.broadcast_to(lanes_of(firsts + seconds)[None], row_ref.shape)


def hidden_grad(sums_ref, slope_ref, normed_ref, inv_ref, out_ref):
    means = jnp.sum(sums_ref[...], axis=0, keepdims=True) * (1.0 / COUNT)
    values = []
    for g in range(4):
        rows = slice(8 * g, 8 * g + 8)
        inv = lane_of(inv_ref[...], g)
        inner = slope_ref[rows, :] - lane_of(means, g) - normed_ref[rows, :] * lane_of(means, 4 + g)
        values.append(inv * inner)
    out_ref[...] = jnp.concatenate(values, axis=0).astype(BF16)


def third_conv(place_ref, g_ref, w_ref, cols_ref, pack_ref, before_ref, column_ref, own_ref, other_ref, factor_ref, normed_ref, row_ref):
    frames = [
        g_ref[:, :, frame * IMG : frame * IMG + IMG].reshape(CH, IMG) for frame in range(2)
    ]
    convolve(frames, w_ref, NN, False, cols_ref, own_ref, other_ref)
    gain, shift = column_ref[:, 0:1], column_ref[:, 1:2]
    mean, inv = column_ref[:, 4:5], column_ref[:, 5:6]
    normed = (pack_ref[OWN:, :].astype(F32) - mean) * inv
    factor = silu_slope(normed * gain + shift) * gain
    normed_before = (before_ref[OWN:, :].astype(F32) - mean) * inv
    factor_before = silu_slope(normed_before * gain + shift) * gain
    factor_ref[...] = factor
    normed_ref[...] = normed
    slope = own_ref[...] * factor
    slope_before = jnp.where(place_ref[1] > 0, other_ref[...].astype(F32) * factor_before, 0.0)
    first = slope + slope_before
    second = slope * normed + slope_before * normed_before
    sums = lanes_of([total_of(value[8 * g : 8 * g + 8]) for value in (first, second) for g in range(4)])
    row_ref[...] = jnp.broadcast_to(sums[None], row_ref.shape)


def own_slope(own_ref, factor_ref, slope_ref):
    slope_ref[...] = own_ref[...] * factor_ref[...]


def input_grad(sums_ref, slope_ref, got_ref, factor_ref, normed_ref, column_ref, grad_ref, out_ref):
    means = jnp.sum(sums_ref[...], axis=0, keepdims=True) * (1.0 / COUNT)
    border = got_ref[...].astype(F32)
    values = []
    for g in range(4):
        rows = slice(8 * g, 8 * g + 8)
        slope = slope_ref[rows, :] + border[rows] * factor_ref[rows, :]
        inner = slope - lane_of(means, g) - normed_ref[rows, :] * lane_of(means, 4 + g)
        values.append(grad_ref[rows, :] + column_ref[rows, 5:6] * inner)
    value = jnp.concatenate(values, axis=0)
    for frame in range(2):
        image = value[:, frame * IMG : frame * IMG + IMG]
        for owner in range(8):
            moved = pltpu.roll(image, (-owner * PART) % IMG, 1) if owner else image
            out_ref[owner, :, frame * 128 : frame * 128 + 128] = moved[:, :128].astype(BF16)


def gather_rows(got_ref, out_ref):
    order = order_matrix()
    for frame in range(2):
        value = got_ref[:, :, frame * 128 : frame * 128 + 128].reshape(CH, 128)
        out_ref[frame * PART : frame * PART + PART, :] = mm(value, order, TN)[:PART].astype(BF16)


def on_device(inputs, grad_out, conv1_weight, conv2_weight, gain1, shift1, gain2, shift2):
    x = inputs.reshape(SHARD, CH)
    upstream = grad_out.reshape(SHARD, CH)
    place = jnp.stack([lax.axis_index("height"), lax.axis_index("tm")]).astype(jnp.int32)
    cols = jnp.asarray(np.arange(IMG)[None, :] % COLS, jnp.int32)
    zero = jnp.zeros_like(gain1)
    vectors = jnp.stack([gain1, shift1, gain2, shift2, zero, zero, zero, zero])
    half = shape(OWN, POS)
    rows16 = shape(16, 1, 128)
    half16 = shape(OWN, POS, dtype=BF16)

    parcel, both = call(
        opening,
        [shape(8, 2 * SHARD + 32, CH, dtype=BF16), shape(54, 8, CH, dtype=BF16)],
        x, upstream, conv1_weight.reshape(27, 8, CH), conv2_weight.reshape(27, 8, CH), vmem_mib=60,
    )
    all_rows = lax.all_to_all(parcel, "height", 0, 0, tiled=True)
    both = lax.all_gather(both.reshape(432, CH), "dp")
    w1_back = call(order_weight, shape(864, CH, dtype=BF16), by_tap(both[:, 216:]))
    w2_back = by_tap(both[:, :216])
    stats1 = call(first_stats, rows16, all_rows)
    all_rows, stats1 = lax.optimization_barrier((all_rows, stats1))
    pieces = call(first_pieces, shape(CH, CH, dtype=BF16), all_rows, flops=3 * 10**10)
    stats1 = exchanged(stats1, 10)
    pieces = lax.all_gather(pieces, "dp")
    pieces = pieces.reshape(4, 8, 4, 8, 2, 128).transpose(4, 2, 0, 1, 3, 5).reshape(8, CH, 128)
    w1_forward = call(turn_weight, shape(896, CH, dtype=BF16), pieces)
    own, pack, columns = call(
        first_conv, [half, shape(2 * OWN, POS, dtype=BF16), shape(OWN, 8)], place, stats1, all_rows, w1_forward, vectors, cols, smem=1
    )
    before = to_later(pack)
    w2_back, _ = lax.optimization_barrier((w2_back, columns))
    own2, other2, grad_t = call(second_conv, [half, half16, half], place, all_rows, w2_back, cols, smem=1)
    hidden, stats2 = call(hidden_stats, [half16, rows16], own, before)
    stats2, other2, hidden = lax.optimization_barrier((stats2, other2, hidden))
    got2 = to_earlier(other2)
    stats2 = exchanged(stats2, 2)
    hidden = call(widen, half, hidden, flops=3 * 10**10)
    slope2, normed2, inv2, sums2 = call(
        second_slope, [half, half, shape(1, 128), rows16], stats2, hidden, own2, got2, columns
    )
    sums2 = exchanged(sums2, 6)
    grad_hidden = call(hidden_grad, half16, sums2, slope2, normed2, inv2)
    grad_hidden = lax.all_gather(grad_hidden, "height")
    own, other, factor1, normed1, sums1 = call(
        third_conv, [half, half16, half, half, rows16], place, grad_hidden, w1_back, cols, pack, before, columns, smem=1
    )
    sums1, other, own = lax.optimization_barrier((sums1, other, own))
    got = to_earlier(other)
    sums1 = exchanged(sums1, 6)
    slope1 = call(own_slope, half, own, factor1, flops=3 * 10**10)
    result = call(
        input_grad, shape(8, OWN, 256, dtype=BF16), sums1, slope1, got, factor1, normed1, columns, grad_t
    )
    result = lax.all_to_all(result, "height", 0, 0, tiled=True)
    return call(gather_rows, shape(SHARD, CH, dtype=BF16), result).reshape(inputs.shape)


def solution(mesh):
    return jax.shard_map(
        on_device,
        mesh=mesh,
        in_specs=(
            P("dp", "tm", "height", None, None),
            P("dp", "tm", "height", None, None),
            P(None, None, ("dp", "height"), None),
            P(None, None, ("dp", "height"), None),
            P(),
            P(),
            P(),
            P(),
        ),
        out_specs=P("dp", "tm", "height", None, None),
        check_vma=False,
    )
```

```python
import jax
import jax.numpy as jnp
import numpy as np
from jax import lax
from jax.experimental import pallas as pl
from jax.experimental.pallas import tpu as pltpu
from jax.sharding import PartitionSpec as P

EPS = 1e-06
F32 = jnp.float32
BF16 = jnp.bfloat16
CH = 256
OWN = 32
COLS = 40
IMG = 640
POS = 2 * IMG
SHARD = 160
PART = 80
COUNT = 32 * IMG * 8


def iota(shape, dim):
    return lax.broadcasted_iota(jnp.int32, shape, dim)


def exact(a, b, dims):
    return lax.dot_general(
        a, b, (dims, ((), ())), precision=lax.Precision.HIGHEST, preferred_element_type=F32
    )


def mm(a, b, dims):
    return lax.dot_general(a, b, (dims, ((), ())), preferred_element_type=F32)


NT = ((1,), (1,))
NN = ((1,), (0,))
TN = ((0,), (0,))


def channel_of(index):
    return ((index >> 3) & 3) * 64 + (index >> 5) * 8 + (index & 7)


def order_matrix():
    return (iota((CH, CH), 1) == channel_of(iota((CH, CH), 0))).astype(F32).astype(BF16)


def own_matrix(h):
    place = iota((OWN, CH), 0)
    return (iota((OWN, CH), 1) == (place >> 3) * 64 + h * 8 + (place & 7)).astype(F32)


def call(kernel, outs, *args, smem=0, vmem_mib=32, flops=10**7):
    many = isinstance(outs, (list, tuple))
    specs = [pl.BlockSpec(memory_space=pltpu.SMEM)] * smem
    specs += [pl.BlockSpec(memory_space=pltpu.VMEM)] * (len(args) - smem)
    vmem = pl.BlockSpec(memory_space=pltpu.VMEM)
    return pl.pallas_call(
        kernel,
        out_shape=outs,
        in_specs=specs,
        out_specs=[vmem] * len(outs) if many else vmem,
        compiler_params=pltpu.CompilerParams(vmem_limit_bytes=vmem_mib * 2**20),
        cost_estimate=pl.CostEstimate(flops=flops, bytes_accessed=10**6, transcendentals=0),
    )(*args)


def shape(*dims, dtype=F32):
    return jax.ShapeDtypeStruct(dims, dtype)


def exchanged(rows, first=0):
    size = rows.shape[0]
    order = [(first + i) % size for i in range(size)]
    got = lax.all_to_all(rows, "tm", 0, 0, axis_index_groups=[order] if first else None, tiled=True)
    return got.reshape(size, 128)


def to_later(block):
    size = lax.axis_size("tm")
    return lax.ppermute(block, "tm", [(i, i + 1) for i in range(size - 1)])


def to_earlier(block):
    size = lax.axis_size("tm")
    return lax.ppermute(block, "tm", [(i + 1, i) for i in range(size - 1)])


def by_tap(weight):
    return weight.reshape(4, 27, 8, CH).transpose(1, 0, 2, 3).reshape(864, CH)


def opening(x_ref, g_ref, w_ref, w2_ref, out_ref, both_ref):
    both_ref[:27] = w2_ref[...]
    both_ref[27:] = w_ref[...]
    total = None
    lane = iota((CH, 1024), 1)
    channel = ((lane >> 3) & 3) * 64 + (lane >> 7) * 8 + (lane & 7)
    hit = iota((CH, 1024), 0) == channel
    for a in range(4):
        place = (hit & (((lane >> 5) & 3) == a)).astype(F32).astype(BF16)
        rows = [w_ref[tap].astype(F32) for tap in range(a, 27, 4)]
        rows += [jnp.zeros((8, CH), F32)] * (8 - len(rows))
        term = mm(jnp.concatenate(rows, axis=0).astype(BF16), place, NN)
        total = term if total is None else total + term
    for owner in range(8):
        piece = total[:, owner * 128 : owner * 128 + 128].astype(BF16)
        out_ref[owner, :SHARD, :] = x_ref[...]
        out_ref[owner, SHARD : 2 * SHARD, :] = g_ref[...]
        out_ref[owner, 2 * SHARD :, :128] = piece[:32]
        out_ref[owner, 2 * SHARD :, 128:] = piece[32:]


def first_pieces(x_ref, out_ref):
    out_ref[...] = x_ref[:, 2 * SHARD :, :].reshape(CH, CH)


def group_sums(row):
    lane = iota(row.shape, 1)
    for step in (1, 2, 4):
        row = row + jnp.where((lane & step) == 0, pltpu.roll(row, CH - step, 1), pltpu.roll(row, step, 1))
    return row


def first_stats(x_ref, row_ref):
    frames = [frame_of(x_ref, frame, 0).astype(F32) for frame in range(2)]
    sums = sum(jnp.sum(x, axis=0, keepdims=True) for x in frames)
    mean = group_sums(sums) * (1.0 / (POS * 8))
    squares = group_sums(sum(jnp.sum((x - mean) * (x - mean), axis=0, keepdims=True) for x in frames))
    row = iota((8, CH), 0)
    both = jnp.where(row == 0, mean, jnp.where(row == 1, squares, 0.0))
    pick = (iota((CH, 128), 0) == 8 * iota((CH, 128), 1)).astype(F32)
    both = exact(both, pick, NN)
    both = both[:1] + pltpu.roll(both, 32, 1)[1:2]
    row_ref[...] = jnp.broadcast_to(both[None], row_ref.shape)


def turn_weight(w_ref, out_ref):
    eye = (iota((128, 128), 0) == iota((128, 128), 1)).astype(F32).astype(BF16)
    for part in range(7):
        out_ref[part * 128 : part * 128 + 128, :] = mm(eye, w_ref[part], NT).astype(BF16)


def order_weight(w_ref, out_ref):
    out_ref[...] = mm(w_ref[...], order_matrix(), NT).astype(BF16)


def shifted(value, by, keep):
    return jnp.where(keep, pltpu.roll(value, (-by) % IMG, 1), 0.0)


def fold(taps, sign, cols_ref):
    lane = iota((OWN, IMG), 1)
    col = jnp.broadcast_to(cols_ref[...], (OWN, IMG))
    keep_col = {1: col != COLS - 1, -1: col != 0}
    keep_row = {1: lane < IMG - COLS, -1: lane >= COLS}
    total = None
    for j in range(3):
        line = None
        for k in range(3):
            value = taps[(3 * j + k) * OWN : (3 * j + k + 1) * OWN, :]
            step = sign * (k - 1)
            if step:
                value = shifted(value, step, keep_col[step])
            line = value if line is None else line + value
        step = sign * (j - 1)
        if step:
            line = shifted(line, step * COLS, keep_row[step])
        total = line if total is None else total + line
    return total


def convolve(frames, weight, dims, forward, cols_ref, own_ref, other_ref):
    if forward:
        plan = [(2, [(0, 0), (1, 1)], other_ref, 0), (3, [(1, 0)], other_ref, 1),
                (0, [(0, 2)], own_ref, 0), (1, [(0, 1), (1, 2)], own_ref, 1)]
    else:
        plan = [(-2, [(0, 0)], other_ref, 0), (-1, [(0, 1), (1, 0)], other_ref, 1),
                (0, [(0, 2), (1, 1)], own_ref, 0), (1, [(1, 2)], own_ref, 1)]
    for _, terms, ref, slot in plan:
        taps = None
        for frame, time_tap in terms:
            term = mm(weight[time_tap * 288 : time_tap * 288 + 288, :], frames[frame], dims)
            taps = term if taps is None else taps + term
        value = fold(taps, 1 if forward else -1, cols_ref)
        ref[:OWN, slot * IMG : slot * IMG + IMG] = value.astype(ref.dtype)


def frame_of(ref, frame, base):
    start = base + frame * PART
    return ref[:, start : start + PART, :].reshape(IMG, CH)


def first_conv(h_ref, stats_ref, x_ref, w_ref, vec_ref, cols_ref, own_ref, pack_ref, column_ref):
    stats = stats_ref[...]
    lane = iota((16, 128), 1)
    mean = jnp.sum(stats, axis=0, keepdims=True) * (1.0 / 16)
    off = stats - mean
    spread_sum = jnp.sum(jnp.where(lane < 32, off * off * (POS * 8.0), stats), axis=0, keepdims=True)
    row = iota((8, 128), 0)
    lane8 = iota((8, 128), 1)
    both = jnp.where(row == 0, jnp.where(lane8 < 32, mean, 0.0), jnp.where(lane8 < 64, spread_sum, 0.0))
    expand = ((iota((128, CH), 0) & 31) == (iota((128, CH), 1) >> 3)).astype(F32)
    wide = exact(both, expand, NN)
    mean_c = wide[0:1]
    inv_c = lax.rsqrt(wide[1:2] * (1.0 / COUNT) + EPS)
    gain, shift = vec_ref[0:1], vec_ref[1:2]
    own = own_matrix(h_ref[0])
    row8 = iota((8, CH), 0)
    vectors = jnp.where(row8 == 4, mean_c, jnp.where(row8 == 5, inv_c, vec_ref[...]))
    columns = exact(own, vectors, NT)
    column_ref[...] = columns
    own16 = own.astype(BF16)
    acts = []
    for frame in range(2):
        raw = frame_of(x_ref, frame, 0)
        pack_ref[OWN:, frame * IMG : frame * IMG + IMG] = mm(own16, raw, NT).astype(BF16)
        pre = (raw.astype(F32) - mean_c) * inv_c * gain + shift
        acts.append((pre * jax.nn.sigmoid(pre)).astype(BF16))
    convolve(acts, w_ref, NT, True, cols_ref, own_ref, pack_ref)


def lanes_of(values):
    lane = iota((1, 128), 1)
    row = jnp.zeros((1, 128), F32)
    for n, value in enumerate(values):
        row = jnp.where(lane == n, value, row)
    return row


def lane_of(row, n):
    return jnp.sum(jnp.where(iota((1, 128), 1) == n, row, 0.0), axis=1, keepdims=True)


def total_of(value):
    return jnp.sum(jnp.sum(value, axis=1, keepdims=True), axis=0, keepdims=True)


def hidden_stats(own_ref, got_ref, hidden_ref, row_ref):
    hidden = (own_ref[...] + got_ref[:OWN, :].astype(F32)).astype(BF16)
    hidden_ref[...] = hidden
    means, spreads = [], []
    for g in range(4):
        value = hidden.astype(F32)[8 * g : 8 * g + 8]
        mean = total_of(value) * (1.0 / (8 * POS))
        off = value - mean
        means.append(mean)
        spreads.append(total_of(off * off))
    row_ref[...] = jnp.broadcast_to(lanes_of(means + spreads)[None], row_ref.shape)


def silu_slope(value):
    sigma = jax.nn.sigmoid(value)
    return sigma * (1.0 + value * (1.0 - sigma))


def second_conv(h_ref, g_ref, w_ref, cols_ref, own_ref, other_ref, grad_ref):
    own16 = own_matrix(h_ref[0]).astype(BF16)
    frames = [frame_of(g_ref, frame, SHARD) for frame in range(2)]
    convolve(frames, w_ref, NT, False, cols_ref, own_ref, other_ref)
    for frame in range(2):
        grad_ref[:, frame * IMG : frame * IMG + IMG] = mm(own16, frames[frame], NT)


def second_slope(stats_ref, hidden_ref, own_ref, got_ref, column_ref, slope_ref, normed_ref, inv_ref, row_ref):
    stats = stats_ref[...]
    mean_row = jnp.sum(stats, axis=0, keepdims=True) * (1.0 / 16)
    off = stats - mean_row
    between = jnp.sum(off * off, axis=0, keepdims=True) * (8.0 * POS)
    within = jnp.sum(stats, axis=0, keepdims=True)
    hidden = hidden_ref[...].astype(F32)
    grad = own_ref[...] + got_ref[...].astype(F32)
    firsts, seconds, invs = [], [], []
    for g in range(4):
        rows = slice(8 * g, 8 * g + 8)
        mean = lane_of(mean_row, g)
        inv = lax.rsqrt((lane_of(between, g) + lane_of(within, 4 + g)) * (1.0 / COUNT) + EPS)
        gain, shift = column_ref[rows, 2:3], column_ref[rows, 3:4]
        normed = (hidden[rows] - mean) * inv
        slope = grad[rows] * silu_slope(normed * gain + shift) * gain
        slope_ref[rows, :] = slope
        normed_ref[rows, :] = normed
        firsts.append(total_of(slope))
        seconds.append(total_of(slope * normed))
        invs.append(inv)
    inv_ref[...] = lanes_of(invs)
    row_ref[...] = jnp.broadcast_to(lanes_of(firsts + seconds)[None], row_ref.shape)


def hidden_grad(sums_ref, slope_ref, normed_ref, inv_ref, out_ref):
    means = jnp.sum(sums_ref[...], axis=0, keepdims=True) * (1.0 / COUNT)
    values = []
    for g in range(4):
        rows = slice(8 * g, 8 * g + 8)
        inv = lane_of(inv_ref[...], g)
        inner = slope_ref[rows, :] - lane_of(means, g) - normed_ref[rows, :] * lane_of(means, 4 + g)
        values.append(inv * inner)
    out_ref[...] = jnp.concatenate(values, axis=0).astype(BF16)


def third_conv(place_ref, g_ref, w_ref, cols_ref, pack_ref, before_ref, column_ref, own_ref, other_ref, factor_ref, normed_ref, row_ref):
    frames = [
        g_ref[:, :, frame * IMG : frame * IMG + IMG].reshape(CH, IMG) for frame in range(2)
    ]
    convolve(frames, w_ref, NN, False, cols_ref, own_ref, other_ref)
    gain, shift = column_ref[:, 0:1], column_ref[:, 1:2]
    mean, inv = column_ref[:, 4:5], column_ref[:, 5:6]
    normed = (pack_ref[OWN:, :].astype(F32) - mean) * inv
    factor = silu_slope(normed * gain + shift) * gain
    normed_before = (before_ref[OWN:, :].astype(F32) - mean) * inv
    factor_before = silu_slope(normed_before * gain + shift) * gain
    factor_ref[...] = factor
    normed_ref[...] = normed
    slope = own_ref[...] * factor
    slope_before = jnp.where(place_ref[1] > 0, other_ref[...].astype(F32) * factor_before, 0.0)
    first = slope + slope_before
    second = slope * normed + slope_before * normed_before
    sums = lanes_of([total_of(value[8 * g : 8 * g + 8]) for value in (first, second) for g in range(4)])
    row_ref[...] = jnp.broadcast_to(sums[None], row_ref.shape)


def own_slope(own_ref, factor_ref, slope_ref):
    slope_ref[...] = own_ref[...] * factor_ref[...]


def input_grad(sums_ref, slope_ref, got_ref, factor_ref, normed_ref, column_ref, grad_ref, out_ref):
    means = jnp.sum(sums_ref[...], axis=0, keepdims=True) * (1.0 / COUNT)
    border = got_ref[...].astype(F32)
    values = []
    for g in range(4):
        rows = slice(8 * g, 8 * g + 8)
        slope = slope_ref[rows, :] + border[rows] * factor_ref[rows, :]
        inner = slope - lane_of(means, g) - normed_ref[rows, :] * lane_of(means, 4 + g)
        values.append(grad_ref[rows, :] + column_ref[rows, 5:6] * inner)
    value = jnp.concatenate(values, axis=0)
    for frame in range(2):
        image = value[:, frame * IMG : frame * IMG + IMG]
        for owner in range(8):
            moved = pltpu.roll(image, (-owner * PART) % IMG, 1) if owner else image
            out_ref[owner, :, frame * 128 : frame * 128 + 128] = moved[:, :128].astype(BF16)


def gather_rows(got_ref, out_ref):
    order = order_matrix()
    for frame in range(2):
        value = got_ref[:, :, frame * 128 : frame * 128 + 128].reshape(CH, 128)
        out_ref[frame * PART : frame * PART + PART, :] = mm(value, order, TN)[:PART].astype(BF16)


def on_device(inputs, grad_out, conv1_weight, conv2_weight, gain1, shift1, gain2, shift2):
    x = inputs.reshape(SHARD, CH)
    upstream = grad_out.reshape(SHARD, CH)
    place = jnp.stack([lax.axis_index("height"), lax.axis_index("tm")]).astype(jnp.int32)
    cols = jnp.asarray(np.arange(IMG)[None, :] % COLS, jnp.int32)
    zero = jnp.zeros_like(gain1)
    vectors = jnp.stack([gain1, shift1, gain2, shift2, zero, zero, zero, zero])
    half = shape(OWN, POS)
    rows16 = shape(16, 1, 128)
    half16 = shape(OWN, POS, dtype=BF16)

    parcel, both = call(
        opening,
        [shape(8, 2 * SHARD + 32, CH, dtype=BF16), shape(54, 8, CH, dtype=BF16)],
        x, upstream, conv1_weight.reshape(27, 8, CH), conv2_weight.reshape(27, 8, CH), vmem_mib=60,
    )
    all_rows = lax.all_to_all(parcel, "height", 0, 0, tiled=True)
    both = lax.all_gather(both.reshape(432, CH), "dp")
    w1_back = call(order_weight, shape(864, CH, dtype=BF16), by_tap(both[:, 216:]))
    w2_back = by_tap(both[:, :216])
    stats1 = call(first_stats, rows16, all_rows)
    all_rows, stats1 = lax.optimization_barrier((all_rows, stats1))
    pieces = call(first_pieces, shape(CH, CH, dtype=BF16), all_rows, flops=3 * 10**10)
    stats1 = exchanged(stats1, 11)
    pieces = lax.all_gather(pieces, "dp")
    pieces = pieces.reshape(4, 8, 4, 8, 2, 128).transpose(4, 2, 0, 1, 3, 5).reshape(8, CH, 128)
    w1_forward = call(turn_weight, shape(896, CH, dtype=BF16), pieces)
    own, pack, columns = call(
        first_conv, [half, shape(2 * OWN, POS, dtype=BF16), shape(OWN, 8)], place, stats1, all_rows, w1_forward, vectors, cols, smem=1
    )
    before = to_later(pack)
    w2_back, _ = lax.optimization_barrier((w2_back, columns))
    own2, other2, grad_t = call(second_conv, [half, half16, half], place, all_rows, w2_back, cols, smem=1)
    got2 = to_earlier(other2)
    hidden, stats2 = call(hidden_stats, [half16, rows16], own, before)
    stats2 = exchanged(stats2, 4)
    slope2, normed2, inv2, sums2 = call(
        second_slope, [half, half, shape(1, 128), rows16], stats2, hidden, own2, got2, columns
    )
    sums2 = exchanged(sums2, 4)
    grad_hidden = call(hidden_grad, half16, sums2, slope2, normed2, inv2)
    grad_hidden = lax.all_gather(grad_hidden, "height")
    own, other, factor1, normed1, sums1 = call(
        third_conv, [half, half16, half, half, rows16], place, grad_hidden, w1_back, cols, pack, before, columns, smem=1
    )
    sums1, other, own = lax.optimization_barrier((sums1, other, own))
    got = to_earlier(other)
    sums1 = exchanged(sums1, 6)
    slope1 = call(own_slope, half, own, factor1, flops=3 * 10**10)
    result = call(
        input_grad, shape(8, OWN, 256, dtype=BF16), sums1, slope1, got, factor1, normed1, columns, grad_t
    )
    result = lax.all_to_all(result, "height", 0, 0, tiled=True)
    return call(gather_rows, shape(SHARD, CH, dtype=BF16), result).reshape(inputs.shape)


def solution(mesh):
    return jax.shard_map(
        on_device,
        mesh=mesh,
        in_specs=(
            P("dp", "tm", "height", None, None),
            P("dp", "tm", "height", None, None),
            P(None, None, ("dp", "height"), None),
            P(None, None, ("dp", "height"), None),
            P(),
            P(),
            P(),
            P(),
        ),
        out_specs=P("dp", "tm", "height", None, None),
        check_vma=False,
    )
```

```python
import jax
import jax.numpy as jnp
import numpy as np
from jax import lax
from jax.experimental import pallas as pl
from jax.experimental.pallas import tpu as pltpu
from jax.sharding import PartitionSpec as P

EPS = 1e-06
F32 = jnp.float32
BF16 = jnp.bfloat16
CH = 256
OWN = 32
COLS = 40
IMG = 640
POS = 2 * IMG
SHARD = 160
PART = 80
COUNT = 32 * IMG * 8


def iota(shape, dim):
    return lax.broadcasted_iota(jnp.int32, shape, dim)


def exact(a, b, dims):
    return lax.dot_general(
        a, b, (dims, ((), ())), precision=lax.Precision.HIGHEST, preferred_element_type=F32
    )


def mm(a, b, dims):
    return lax.dot_general(a, b, (dims, ((), ())), preferred_element_type=F32)


NT = ((1,), (1,))
NN = ((1,), (0,))
TN = ((0,), (0,))


def channel_of(index):
    return ((index >> 3) & 3) * 64 + (index >> 5) * 8 + (index & 7)


def order_matrix():
    return (iota((CH, CH), 1) == channel_of(iota((CH, CH), 0))).astype(F32).astype(BF16)


def own_matrix(h):
    place = iota((OWN, CH), 0)
    return (iota((OWN, CH), 1) == (place >> 3) * 64 + h * 8 + (place & 7)).astype(F32)


def call(kernel, outs, *args, smem=0, vmem_mib=32, flops=10**7):
    many = isinstance(outs, (list, tuple))
    specs = [pl.BlockSpec(memory_space=pltpu.SMEM)] * smem
    specs += [pl.BlockSpec(memory_space=pltpu.VMEM)] * (len(args) - smem)
    vmem = pl.BlockSpec(memory_space=pltpu.VMEM)
    return pl.pallas_call(
        kernel,
        out_shape=outs,
        in_specs=specs,
        out_specs=[vmem] * len(outs) if many else vmem,
        compiler_params=pltpu.CompilerParams(vmem_limit_bytes=vmem_mib * 2**20),
        cost_estimate=pl.CostEstimate(flops=flops, bytes_accessed=10**6, transcendentals=0),
    )(*args)


def shape(*dims, dtype=F32):
    return jax.ShapeDtypeStruct(dims, dtype)


def exchanged(rows, first=0):
    size = rows.shape[0]
    order = [(first + i) % size for i in range(size)]
    got = lax.all_to_all(rows, "tm", 0, 0, axis_index_groups=[order] if first else None, tiled=True)
    return got.reshape(size, 128)


def to_later(block):
    size = lax.axis_size("tm")
    return lax.ppermute(block, "tm", [(i, i + 1) for i in range(size - 1)])


def to_earlier(block):
    size = lax.axis_size("tm")
    return lax.ppermute(block, "tm", [(i + 1, i) for i in range(size - 1)])


def by_tap(weight):
    return weight.reshape(4, 27, 8, CH).transpose(1, 0, 2, 3).reshape(864, CH)


def opening(x_ref, g_ref, w_ref, w2_ref, out_ref, both_ref):
    both_ref[:27] = w2_ref[...]
    both_ref[27:] = w_ref[...]
    total = None
    lane = iota((CH, 1024), 1)
    channel = ((lane >> 3) & 3) * 64 + (lane >> 7) * 8 + (lane & 7)
    hit = iota((CH, 1024), 0) == channel
    for a in range(4):
        place = (hit & (((lane >> 5) & 3) == a)).astype(F32).astype(BF16)
        rows = [w_ref[tap].astype(F32) for tap in range(a, 27, 4)]
        rows += [jnp.zeros((8, CH), F32)] * (8 - len(rows))
        term = mm(jnp.concatenate(rows, axis=0).astype(BF16), place, NN)
        total = term if total is None else total + term
    for owner in range(8):
        piece = total[:, owner * 128 : owner * 128 + 128].astype(BF16)
        out_ref[owner, :SHARD, :] = x_ref[...]
        out_ref[owner, SHARD : 2 * SHARD, :] = g_ref[...]
        out_ref[owner, 2 * SHARD :, :128] = piece[:32]
        out_ref[owner, 2 * SHARD :, 128:] = piece[32:]


def first_pieces(x_ref, out_ref):
    out_ref[...] = x_ref[:, 2 * SHARD :, :].reshape(CH, CH)


def group_sums(row):
    lane = iota(row.shape, 1)
    for step in (1, 2, 4):
        row = row + jnp.where((lane & step) == 0, pltpu.roll(row, CH - step, 1), pltpu.roll(row, step, 1))
    return row


def first_stats(x_ref, row_ref):
    frames = [frame_of(x_ref, frame, 0).astype(F32) for frame in range(2)]
    sums = sum(jnp.sum(x, axis=0, keepdims=True) for x in frames)
    mean = group_sums(sums) * (1.0 / (POS * 8))
    squares = group_sums(sum(jnp.sum((x - mean) * (x - mean), axis=0, keepdims=True) for x in frames))
    row = iota((8, CH), 0)
    both = jnp.where(row == 0, mean, jnp.where(row == 1, squares, 0.0))
    pick = (iota((CH, 128), 0) == 8 * iota((CH, 128), 1)).astype(F32)
    both = exact(both, pick, NN)
    both = both[:1] + pltpu.roll(both, 32, 1)[1:2]
    row_ref[...] = jnp.broadcast_to(both[None], row_ref.shape)


def turn_weight(w_ref, out_ref):
    eye = (iota((128, 128), 0) == iota((128, 128), 1)).astype(F32).astype(BF16)
    for part in range(7):
        out_ref[part * 128 : part * 128 + 128, :] = mm(eye, w_ref[part], NT).astype(BF16)


def order_weight(w_ref, out_ref):
    out_ref[...] = mm(w_ref[...], order_matrix(), NT).astype(BF16)


def shifted(value, by, keep):
    return jnp.where(keep, pltpu.roll(value, (-by) % IMG, 1), 0.0)


def fold(taps, sign, cols_ref):
    lane = iota((OWN, IMG), 1)
    col = jnp.broadcast_to(cols_ref[...], (OWN, IMG))
    keep_col = {1: col != COLS - 1, -1: col != 0}
    keep_row = {1: lane < IMG - COLS, -1: lane >= COLS}
    total = None
    for j in range(3):
        line = None
        for k in range(3):
            value = taps[(3 * j + k) * OWN : (3 * j + k + 1) * OWN, :]
            step = sign * (k - 1)
            if step:
                value = shifted(value, step, keep_col[step])
            line = value if line is None else line + value
        step = sign * (j - 1)
        if step:
            line = shifted(line, step * COLS, keep_row[step])
        total = line if total is None else total + line
    return total


def convolve(frames, weight, dims, forward, cols_ref, own_ref, other_ref):
    if forward:
        plan = [(2, [(0, 0), (1, 1)], other_ref, 0), (3, [(1, 0)], other_ref, 1),
                (0, [(0, 2)], own_ref, 0), (1, [(0, 1), (1, 2)], own_ref, 1)]
    else:
        plan = [(-2, [(0, 0)], other_ref, 0), (-1, [(0, 1), (1, 0)], other_ref, 1),
                (0, [(0, 2), (1, 1)], own_ref, 0), (1, [(1, 2)], own_ref, 1)]
    for _, terms, ref, slot in plan:
        taps = None
        for frame, time_tap in terms:
            term = mm(weight[time_tap * 288 : time_tap * 288 + 288, :], frames[frame], dims)
            taps = term if taps is None else taps + term
        value = fold(taps, 1 if forward else -1, cols_ref)
        ref[:OWN, slot * IMG : slot * IMG + IMG] = value.astype(ref.dtype)


def frame_of(ref, frame, base):
    start = base + frame * PART
    return ref[:, start : start + PART, :].reshape(IMG, CH)


def first_conv(h_ref, stats_ref, x_ref, w_ref, vec_ref, cols_ref, own_ref, pack_ref, column_ref):
    stats = stats_ref[...]
    lane = iota((16, 128), 1)
    mean = jnp.sum(stats, axis=0, keepdims=True) * (1.0 / 16)
    off = stats - mean
    spread_sum = jnp.sum(jnp.where(lane < 32, off * off * (POS * 8.0), stats), axis=0, keepdims=True)
    row = iota((8, 128), 0)
    lane8 = iota((8, 128), 1)
    both = jnp.where(row == 0, jnp.where(lane8 < 32, mean, 0.0), jnp.where(lane8 < 64, spread_sum, 0.0))
    expand = ((iota((128, CH), 0) & 31) == (iota((128, CH), 1) >> 3)).astype(F32)
    wide = exact(both, expand, NN)
    mean_c = wide[0:1]
    inv_c = lax.rsqrt(wide[1:2] * (1.0 / COUNT) + EPS)
    gain, shift = vec_ref[0:1], vec_ref[1:2]
    own = own_matrix(h_ref[0])
    row8 = iota((8, CH), 0)
    vectors = jnp.where(row8 == 4, mean_c, jnp.where(row8 == 5, inv_c, vec_ref[...]))
    columns = exact(own, vectors, NT)
    column_ref[...] = columns
    own16 = own.astype(BF16)
    acts = []
    for frame in range(2):
        raw = frame_of(x_ref, frame, 0)
        pack_ref[OWN:, frame * IMG : frame * IMG + IMG] = mm(own16, raw, NT).astype(BF16)
        pre = (raw.astype(F32) - mean_c) * inv_c * gain + shift
        acts.append((pre * jax.nn.sigmoid(pre)).astype(BF16))
    convolve(acts, w_ref, NT, True, cols_ref, own_ref, pack_ref)


def lanes_of(values):
    lane = iota((1, 128), 1)
    row = jnp.zeros((1, 128), F32)
    for n, value in enumerate(values):
        row = jnp.where(lane == n, value, row)
    return row


def lane_of(row, n):
    return jnp.sum(jnp.where(iota((1, 128), 1) == n, row, 0.0), axis=1, keepdims=True)


def total_of(value):
    return jnp.sum(jnp.sum(value, axis=1, keepdims=True), axis=0, keepdims=True)


def hidden_stats(own_ref, got_ref, hidden_ref, row_ref):
    hidden = (own_ref[...] + got_ref[:OWN, :].astype(F32)).astype(BF16)
    hidden_ref[...] = hidden
    means, spreads = [], []
    for g in range(4):
        value = hidden.astype(F32)[8 * g : 8 * g + 8]
        mean = total_of(value) * (1.0 / (8 * POS))
        off = value - mean
        means.append(mean)
        spreads.append(total_of(off * off))
    row_ref[...] = jnp.broadcast_to(lanes_of(means + spreads)[None], row_ref.shape)


def silu_slope(value):
    sigma = jax.nn.sigmoid(value)
    return sigma * (1.0 + value * (1.0 - sigma))


def second_conv(h_ref, g_ref, w_ref, cols_ref, own_ref, other_ref, grad_ref):
    own16 = own_matrix(h_ref[0]).astype(BF16)
    frames = [frame_of(g_ref, frame, SHARD) for frame in range(2)]
    convolve(frames, w_ref, NT, False, cols_ref, own_ref, other_ref)
    for frame in range(2):
        grad_ref[:, frame * IMG : frame * IMG + IMG] = mm(own16, frames[frame], NT)


def second_slope(stats_ref, hidden_ref, own_ref, got_ref, column_ref, slope_ref, normed_ref, inv_ref, row_ref):
    stats = stats_ref[...]
    mean_row = jnp.sum(stats, axis=0, keepdims=True) * (1.0 / 16)
    off = stats - mean_row
    between = jnp.sum(off * off, axis=0, keepdims=True) * (8.0 * POS)
    within = jnp.sum(stats, axis=0, keepdims=True)
    hidden = hidden_ref[...].astype(F32)
    grad = own_ref[...] + got_ref[...].astype(F32)
    firsts, seconds, invs = [], [], []
    for g in range(4):
        rows = slice(8 * g, 8 * g + 8)
        mean = lane_of(mean_row, g)
        inv = lax.rsqrt((lane_of(between, g) + lane_of(within, 4 + g)) * (1.0 / COUNT) + EPS)
        gain, shift = column_ref[rows, 2:3], column_ref[rows, 3:4]
        normed = (hidden[rows] - mean) * inv
        slope = grad[rows] * silu_slope(normed * gain + shift) * gain
        slope_ref[rows, :] = slope
        normed_ref[rows, :] = normed
        firsts.append(total_of(slope))
        seconds.append(total_of(slope * normed))
        invs.append(inv)
    inv_ref[...] = lanes_of(invs)
    row_ref[...] = jnp.broadcast_to(lanes_of(firsts + seconds)[None], row_ref.shape)


def hidden_grad(sums_ref, slope_ref, normed_ref, inv_ref, out_ref):
    means = jnp.sum(sums_ref[...], axis=0, keepdims=True) * (1.0 / COUNT)
    values = []
    for g in range(4):
        rows = slice(8 * g, 8 * g + 8)
        inv = lane_of(inv_ref[...], g)
        inner = slope_ref[rows, :] - lane_of(means, g) - normed_ref[rows, :] * lane_of(means, 4 + g)
        values.append(inv * inner)
    out_ref[...] = jnp.concatenate(values, axis=0).astype(BF16)


def third_conv(place_ref, g_ref, w_ref, cols_ref, pack_ref, before_ref, column_ref, own_ref, other_ref, factor_ref, normed_ref, row_ref):
    frames = [
        g_ref[:, :, frame * IMG : frame * IMG + IMG].reshape(CH, IMG) for frame in range(2)
    ]
    convolve(frames, w_ref, NN, False, cols_ref, own_ref, other_ref)
    gain, shift = column_ref[:, 0:1], column_ref[:, 1:2]
    mean, inv = column_ref[:, 4:5], column_ref[:, 5:6]
    normed = (pack_ref[OWN:, :].astype(F32) - mean) * inv
    factor = silu_slope(normed * gain + shift) * gain
    normed_before = (before_ref[OWN:, :].astype(F32) - mean) * inv
    factor_before = silu_slope(normed_before * gain + shift) * gain
    factor_ref[...] = factor
    normed_ref[...] = normed
    slope = own_ref[...] * factor
    slope_before = jnp.where(place_ref[1] > 0, other_ref[...].astype(F32) * factor_before, 0.0)
    first = slope + slope_before
    second = slope * normed + slope_before * normed_before
    sums = lanes_of([total_of(value[8 * g : 8 * g + 8]) for value in (first, second) for g in range(4)])
    row_ref[...] = jnp.broadcast_to(sums[None], row_ref.shape)


def own_slope(own_ref, factor_ref, slope_ref):
    slope_ref[...] = own_ref[...] * factor_ref[...]


def input_grad(sums_ref, slope_ref, got_ref, factor_ref, normed_ref, column_ref, grad_ref, out_ref):
    means = jnp.sum(sums_ref[...], axis=0, keepdims=True) * (1.0 / COUNT)
    border = got_ref[...].astype(F32)
    values = []
    for g in range(4):
        rows = slice(8 * g, 8 * g + 8)
        slope = slope_ref[rows, :] + border[rows] * factor_ref[rows, :]
        inner = slope - lane_of(means, g) - normed_ref[rows, :] * lane_of(means, 4 + g)
        values.append(grad_ref[rows, :] + column_ref[rows, 5:6] * inner)
    value = jnp.concatenate(values, axis=0)
    for frame in range(2):
        image = value[:, frame * IMG : frame * IMG + IMG]
        for owner in range(8):
            moved = pltpu.roll(image, (-owner * PART) % IMG, 1) if owner else image
            out_ref[owner, :, frame * 128 : frame * 128 + 128] = moved[:, :128].astype(BF16)


def gather_rows(got_ref, out_ref):
    order = order_matrix()
    for frame in range(2):
        value = got_ref[:, :, frame * 128 : frame * 128 + 128].reshape(CH, 128)
        out_ref[frame * PART : frame * PART + PART, :] = mm(value, order, TN)[:PART].astype(BF16)


def on_device(inputs, grad_out, conv1_weight, conv2_weight, gain1, shift1, gain2, shift2):
    x = inputs.reshape(SHARD, CH)
    upstream = grad_out.reshape(SHARD, CH)
    place = jnp.stack([lax.axis_index("height"), lax.axis_index("tm")]).astype(jnp.int32)
    cols = jnp.asarray(np.arange(IMG)[None, :] % COLS, jnp.int32)
    zero = jnp.zeros_like(gain1)
    vectors = jnp.stack([gain1, shift1, gain2, shift2, zero, zero, zero, zero])
    half = shape(OWN, POS)
    rows16 = shape(16, 1, 128)
    half16 = shape(OWN, POS, dtype=BF16)

    parcel, both = call(
        opening,
        [shape(8, 2 * SHARD + 32, CH, dtype=BF16), shape(54, 8, CH, dtype=BF16)],
        x, upstream, conv1_weight.reshape(27, 8, CH), conv2_weight.reshape(27, 8, CH), vmem_mib=60,
    )
    all_rows = lax.all_to_all(parcel, "height", 0, 0, tiled=True)
    both = lax.all_gather(both.reshape(432, CH), "dp")
    w1_back = call(order_weight, shape(864, CH, dtype=BF16), by_tap(both[:, 216:]))
    w2_back = by_tap(both[:, :216])
    stats1 = call(first_stats, rows16, all_rows)
    all_rows, stats1 = lax.optimization_barrier((all_rows, stats1))
    pieces = call(first_pieces, shape(CH, CH, dtype=BF16), all_rows, flops=3 * 10**10)
    stats1 = exchanged(stats1, 11)
    pieces = lax.all_gather(pieces, "dp")
    pieces = pieces.reshape(4, 8, 4, 8, 2, 128).transpose(4, 2, 0, 1, 3, 5).reshape(8, CH, 128)
    w1_forward = call(turn_weight, shape(896, CH, dtype=BF16), pieces)
    own, pack, columns = call(
        first_conv, [half, shape(2 * OWN, POS, dtype=BF16), shape(OWN, 8)], place, stats1, all_rows, w1_forward, vectors, cols, smem=1
    )
    before = to_later(pack)
    w2_back, _ = lax.optimization_barrier((w2_back, columns))
    own2, other2, grad_t = call(second_conv, [half, half16, half], place, all_rows, w2_back, cols, smem=1)
    got2 = to_earlier(other2)
    hidden, stats2 = call(hidden_stats, [half16, rows16], own, before)
    stats2 = exchanged(stats2, 4)
    slope2, normed2, inv2, sums2 = call(
        second_slope, [half, half, shape(1, 128), rows16], stats2, hidden, own2, got2, columns
    )
    sums2 = exchanged(sums2, 4)
    grad_hidden = call(hidden_grad, half16, sums2, slope2, normed2, inv2)
    grad_hidden = lax.all_gather(grad_hidden, "height")
    own, other, factor1, normed1, sums1 = call(
        third_conv, [half, half16, half, half, rows16], place, grad_hidden, w1_back, cols, pack, before, columns, smem=1
    )
    sums1, other, own = lax.optimization_barrier((sums1, other, own))
    got = to_earlier(other)
    sums1 = exchanged(sums1, 4)
    slope1 = call(own_slope, half, own, factor1, flops=3 * 10**10)
    result = call(
        input_grad, shape(8, OWN, 256, dtype=BF16), sums1, slope1, got, factor1, normed1, columns, grad_t
    )
    result = lax.all_to_all(result, "height", 0, 0, tiled=True)
    return call(gather_rows, shape(SHARD, CH, dtype=BF16), result).reshape(inputs.shape)


def solution(mesh):
    return jax.shard_map(
        on_device,
        mesh=mesh,
        in_specs=(
            P("dp", "tm", "height", None, None),
            P("dp", "tm", "height", None, None),
            P(None, None, ("dp", "height"), None),
            P(None, None, ("dp", "height"), None),
            P(),
            P(),
            P(),
            P(),
        ),
        out_specs=P("dp", "tm", "height", None, None),
        check_vma=False,
    )
```
